32 devices in a mesh: dp: 2 (over x), row: 4 (over y, core), col: 4 (over z).
Axes of the slice: x: 2, y: 2, z: 4, core: 2. Of those that a mesh axis runs over, the one named last changes fastest.
Arguments:
- tokens: bfloat16 [896, 4096], P(('dp', 'col'), 'row'), may hold values from -6 to 6
- gate_up: bfloat16 [2, 4096, 14336], P(None, 'row', ('dp', 'col')), may hold values from -0.09375 to 0.09375
- down_weight: bfloat16 [14336, 4096], P(('dp', 'col'), 'row'), may hold values from -0.046875 to 0.046875
Outputs:
- mixed: bfloat16 [896, 4096], P(('dp', 'col'), 'row')
- col_check: float32 [4096], P('row')
- row_check: float32 [896], P(('dp', 'col'))
The draws below stay inside these ranges and needn't reach their ends.
All inputs are finite; a program needn't handle non-finite values.
Results may differ from the reference program's by a relative error of at most 0.0049.
Values may be sent and summed in bfloat16 or wider, within the bound.
A program may use at most 128 MiB of HBM per device.

```python
import math
import jax
import jax.numpy as jnp
from jax import lax

D = 4096
FF = 14336
TOKENS = 896


def shard_levels(stream_key, dims, shards, least, top_value):
    gain = 1.0
    for dim, shards_of in shards:
        draws = jax.random.uniform(jax.random.fold_in(jax.random.fold_in(stream_key, 6), dim), (shards_of,), jnp.float32, least / len(shards), top_value / len(shards))
        gain = gain * jnp.repeat(jnp.exp(draws), dims[dim] // shards_of).reshape((-1,) + (1,) * (len(dims) - 1 - dim))
    return gain


def gaussian(own_key, extent, width, reach, cuts=(), dtype=jnp.bfloat16):
    array = jax.random.normal(own_key, extent, jnp.float32) * width
    if len(cuts) > 0:
        array = shard_levels(own_key, extent, cuts, -0.22, 0.18) * array
    return jnp.clip(array, min=-reach, max=reach).astype(dtype)


def setup_inputs(seed: int = 0) -> dict:
    keys = jax.random.split(jax.random.key(seed), 4)
    tokens = gaussian(keys[0], (TOKENS, D), 1.0, 6.0, ((0, 8), (1, 4)))
    gate_up = gaussian(keys[1], (2, D, FF), D ** -0.5, 0.09375, ((1, 4), (2, 8)))
    down_weight = gaussian(keys[2], (FF, D), FF ** -0.5, 0.046875, ((0, 8), (1, 4)))
    return dict(tokens=tokens, gate_up=gate_up, down_weight=down_weight)


def reference(tokens, gate_up, down_weight):
    gate = jnp.dot(tokens, gate_up[0], preferred_element_type=jnp.float32)
    up = jnp.dot(tokens, gate_up[1], preferred_element_type=jnp.float32)
    hidden = (jax.nn.silu(gate) * up).astype(jnp.bfloat16)
    mixed = jnp.dot(hidden, down_weight, preferred_element_type=jnp.float32).astype(jnp.bfloat16)
    hidden_wide = hidden.astype(jnp.float32)
    weight_wide = down_weight.astype(jnp.float32)
    unit_sums = lax.optimization_barrier(jnp.sum(hidden_wide, axis=0))
    col_check = jnp.dot(unit_sums, weight_wide, precision=lax.Precision.HIGHEST) / math.sqrt(TOKENS)
    weight_sums = lax.optimization_barrier(jnp.sum(weight_wide, axis=1))
    row_check = jnp.dot(hidden_wide, weight_sums, precision=lax.Precision.HIGHEST) / math.sqrt(D)
    return (mixed, col_check, row_check)
```

```python
import functools
import math

import jax
import jax.numpy as jnp
from jax import lax
from jax.experimental import pallas as pl
from jax.experimental.pallas import tpu as pltpu
from jax.sharding import PartitionSpec as P

MESH = pl.DeviceIdType.MESH
TILE = 256


def swiglu(partial_value):
    return (jax.nn.silu(partial_value[:, 0]) * partial_value[:, 1]).astype(jnp.bfloat16)


def hidden_units(partial_value):
    share = lax.psum_scatter(partial_value, "row", scatter_dimension=0, tiled=True)
    return lax.all_gather(swiglu(share), "row", axis=0, tiled=True)


def make_accumulate(hidden, shard_piece):
    columns_wide = hidden.astype(jnp.float32)
    piece_wide = shard_piece.astype(jnp.float32)
    output_part = jnp.dot(hidden, shard_piece, preferred_element_type=jnp.float32)
    column_part = jnp.dot(
        jnp.sum(columns_wide, axis=0), piece_wide, precision=lax.Precision.HIGHEST
    )
    row_part = jnp.dot(columns_wide, jnp.sum(piece_wide, axis=1), precision=lax.Precision.HIGHEST)
    return (output_part, column_part, row_part)


def per_device(tokens, gate_up, down_weight):
    total_tokens = tokens.shape[0] * lax.axis_size(("dp", "col"))
    model_width = tokens.shape[1] * lax.axis_size("row")
    group_rows = lax.all_gather(tokens, "col", axis=0, tiled=True)
    partial_value = jnp.einsum(
        "td,gdf->tgf",
        group_rows,
        lax.all_gather(gate_up, "dp", axis=2, tiled=True),
        preferred_element_type=jnp.float32,
    )
    hidden = hidden_units(partial_value)
    output_part, column_part, row_part = make_accumulate(
        hidden, lax.all_gather(down_weight, "dp", axis=0, tiled=True)
    )
    mixed, row_share = (
        lax.psum_scatter(output_part, "col", scatter_dimension=0, tiled=True),
        lax.psum_scatter(row_part, "col", scatter_dimension=0, tiled=True),
    )
    col_check = lax.psum(column_part, ("dp", "col")) / math.sqrt(total_tokens)
    row_check = lax.psum(row_share, "row") / math.sqrt(model_width)
    return (mixed.astype(jnp.bfloat16), col_check, row_check)


def dot(a, b):
    return jnp.dot(a, b, preferred_element_type=jnp.float32)


def dot_rows(a, b):
    return lax.dot_general(a, b, (((1,), (1,)), ((), ())), preferred_element_type=jnp.float32)


def three_terms(row):
    high = row.astype(jnp.bfloat16)
    rest = row - high.astype(jnp.float32)
    middle = rest.astype(jnp.bfloat16)
    low = (rest - middle.astype(jnp.float32)).astype(jnp.bfloat16)
    index = lax.broadcasted_iota(jnp.int32, row.shape, 0)
    terms = jnp.where(
        index == 0,
        high.astype(jnp.float32),
        jnp.where(
            index == 1,
            middle.astype(jnp.float32),
            jnp.where(index == 2, low.astype(jnp.float32), 0.0),
        ),
    )
    return terms.astype(jnp.bfloat16)


def kernel(
    total_tokens,
    model_width,
    tokens_ref,
    gate_up_ref,
    down_ref,
    mixed_ref,
    col_ref,
    row_ref,
    weights,
    down,
    acts,
    part_wide,
    part_send,
    part_recv,
    hidden,
    out_wide,
    out_send,
    x_recv,
    z_send,
    z_recv,
    own_sum,
    unit_sums,
    weight_parts,
    weight_terms,
    small_send,
    small_recv,
    local_sem,
    w_send,
    w_recv,
    tz_send,
    tz_recv,
    tx_send,
    tx_recv,
    tp_send,
    tp_recv,
    py_send,
    py_recv,
    hp_send,
    hp_recv,
    hy_send,
    hy_recv,
    hf_send,
    hf_recv,
    mx_send,
    mx_recv,
    mz_send,
    mz_recv,
    ws_send,
    ws_recv,
    sm_send,
    sm_recv,
):
    block, width = tokens_ref.shape
    units = down_ref.shape[0]
    half = units // 2
    x = lax.axis_index("dp")
    row = lax.axis_index("row")
    z = lax.axis_index("col")
    y, core = lax.div(row, 2), lax.rem(row, 2)
    nx, ny, ncore = 1 - x, 1 - y, 1 - core
    zs = [z, z + 1 - 2 * lax.rem(z, 2), lax.rem(z + 2, 4), 3 - z]
    partner = (x, y * 2 + ncore, z)
    across_y = (x, ny * 2 + core, z)
    across_x = (nx, row, z)
    rows = [(x, lax.rem(row + k, 4), z) for k in range(1, 4)]
    peers = [(x, row, zs[j]) for j in range(1, 4)] + [(nx, row, zs[j]) for j in range(4)]
    small_slots = [(j, x) for j in range(1, 4)] + [(j, nx) for j in range(4)]
    sent = []

    def send(src, dst, send_sem, recv_sem, device):
        copy = pltpu.make_async_remote_copy(
            src_ref=src,
            dst_ref=dst,
            send_sem=send_sem,
            recv_sem=recv_sem,
            device_id=device,
            device_id_type=MESH,
        )
        copy.start()
        sent.append(copy)
        return copy

    def lanes(which):
        return pl.ds(pl.multiple_of(which * half, 128), half)

    local = [
        pltpu.make_async_copy(tokens_ref, acts.at[z, core, x], local_sem.at[0]),
        pltpu.make_async_copy(
            gate_up_ref.at[0, :, lanes(core)], weights.at[core, :, 0:half], local_sem.at[1]
        ),
        pltpu.make_async_copy(
            gate_up_ref.at[1, :, lanes(core)], weights.at[core, :, half:units], local_sem.at[2]
        ),
        pltpu.make_async_copy(down_ref, down, local_sem.at[3]),
    ]
    for copy in local:
        copy.start()

    barrier = pltpu.get_barrier_semaphore()
    for device in rows + peers:
        pl.semaphore_signal(barrier, inc=1, device_id=device, device_id_type=MESH)
    pl.semaphore_wait(barrier, len(rows) + len(peers))

    tx, tp, tz = {}, {}, {}
    tx[0] = send(tokens_ref, acts.at[z, core, x], tx_send.at[0], tx_recv.at[0], across_x)
    tp[0, 0] = send(tokens_ref, acts.at[z, core, x], tp_send.at[0], tp_recv.at[0], partner)
    for j in range(1, 4):
        tz[j] = send(
            tokens_ref, acts.at[z, core, x], tz_send.at[j - 1], tz_recv.at[j - 1], peers[j - 1]
        )
    swap = [
        send(
            gate_up_ref.at[g, :, lanes(ncore)],
            weights.at[core, :, g * half : (g + 1) * half],
            w_send.at[g],
            w_recv.at[g],
            partner,
        )
        for g in range(2)
    ]

    unit_sums[...] = jnp.zeros_like(unit_sums)
    small_send[...] = jnp.zeros_like(small_send)

    local[3].wait()
    ones_width = jnp.ones((8, width), jnp.bfloat16)
    for h in range(2):
        weight_parts[row, h] = dot_rows(ones_width, down[h * half : (h + 1) * half, :])
    weight_copies = [
        send(
            weight_parts.at[row], weight_parts.at[row], ws_send.at[k], ws_recv.at[k], rows[k]
        )
        for k in range(3)
    ]

    def arrive(j):
        tz[j].wait_recv()
        place = acts.at[zs[j], core, x]
        tx[j] = send(place, place, tx_send.at[j], tx_recv.at[j], across_x)
        tp[j, 0] = send(place, place, tp_send.at[2 * j], tp_recv.at[2 * j], partner)

    def arrive_across(j):
        tx[j].wait_recv()
        place = acts.at[zs[j], core, nx]
        tp[j, 1] = send(place, place, tp_send.at[2 * j + 1], tp_recv.at[2 * j + 1], partner)

    py, hp, hy, hf, mx, mz = {}, {}, {}, {}, {}, {}

    def gate_and_up(j):
        tp[j, 0].wait_recv()
        tp[j, 1].wait_recv()

        def body(t, carry):
            columns = pl.ds(pl.multiple_of(t * TILE, TILE), TILE)
            product = dot(
                acts[zs[j], 0].reshape(2 * block, width), weights[0, :, columns]
            ) + dot(acts[zs[j], 1].reshape(2 * block, width), weights[1, :, columns])
            product = product.reshape(2, block, TILE)
            part_wide[j, :, :, columns] = product
            part_send[j, :, :, columns] = product.astype(jnp.bfloat16)
            return carry

        lax.fori_loop(0, units // TILE, body, 0)
        py[j] = send(
            part_send.at[j, ny], part_recv.at[j], py_send.at[j], py_recv.at[j], across_y
        )

    def activate(j):
        py[j].wait_recv()
        gate = part_wide[j, y, :, 0:half] + part_recv[j, :, 0:half].astype(jnp.float32)
        up = part_wide[j, y, :, half:units] + part_recv[j, :, half:units].astype(jnp.float32)
        hidden[j, core, y] = (gate / (1.0 + jnp.exp(-gate)) * up).astype(jnp.bfloat16)
        place = hidden.at[j, core, y]
        hy[j] = send(place, place, hy_send.at[j], hy_recv.at[j], across_y)
        hp[j] = send(place, place, hp_send.at[j], hp_recv.at[j], partner)

    def hand_over(j):
        hy[j].wait_recv()
        place = hidden.at[j, core, ny]
        hf[j] = send(place, place, hf_send.at[j], hf_recv.at[j], partner)

    def down_part(j):
        hp[j].wait_recv()
        hf[j].wait_recv()

        def body(t, carry):
            columns = pl.ds(pl.multiple_of(t * TILE, TILE), TILE)
            product = dot(
                hidden[j, 0].reshape(2 * block, half), down[0:half, columns]
            ) + dot(hidden[j, 1].reshape(2 * block, half), down[half:units, columns])
            product = product.reshape(2, block, TILE)
            out_wide[j, :, :, columns] = product
            out_send[j, :, :, columns] = product.astype(jnp.bfloat16)
            return carry

        lax.fori_loop(0, width // TILE, body, 0)
        mx[j] = send(out_send.at[j, nx], x_recv.at[j], mx_send.at[j], mx_recv.at[j], across_x)

    def checks(j):
        ones = jnp.ones((8, 2 * block), jnp.bfloat16)
        for h in range(2):
            unit_sums[h] += dot(ones, hidden[j, h].reshape(2 * block, half))
        for b in range(2):
            terms = dot_rows(weight_terms[0], hidden[j, 0, b]) + dot_rows(
                weight_terms[1], hidden[j, 1, b]
            )
            small_send[j, b, 8:9, 0:block] = jnp.sum(terms, axis=0, keepdims=True)

    def add_across(j):
        mx[j].wait_recv()
        value = out_wide[j, x] + x_recv[j].astype(jnp.float32)
        if j == 0:
            own_sum[...] = value
        else:
            z_send[j - 1] = value.astype(jnp.bfloat16)
            mz[j] = send(
                z_send.at[j - 1],
                z_recv.at[j - 1],
                mz_send.at[j - 1],
                mz_recv.at[j - 1],
                peers[j - 1],
            )

    arrive_across(0)
    arrive(1)
    for copy in local[:3]:
        copy.wait()
    for copy in swap:
        copy.wait_recv()
    gate_and_up(0)
    arrive_across(1)
    arrive(2)
    gate_and_up(1)
    for copy in weight_copies:
        copy.wait_recv()
    for h in range(2):
        weight_terms[h] = three_terms(
            weight_parts[0, h] + weight_parts[1, h] + weight_parts[2, h] + weight_parts[3, h]
        )
    activate(0)
    arrive_across(2)
    arrive(3)
    gate_and_up(2)
    activate(1)
    hand_over(0)
    arrive_across(3)
    gate_and_up(3)
    hand_over(1)
    down_part(0)
    activate(2)
    down_part(1)
    add_across(0)
    checks(0)
    hand_over(2)
    activate(3)
    add_across(1)
    down_part(2)
    checks(1)
    checks(2)
    hand_over(3)
    add_across(2)
    down_part(3)
    checks(3)

    column_terms = dot(three_terms(unit_sums[0]), down[0:half, :]) + dot(
        three_terms(unit_sums[1]), down[half:units, :]
    )
    columns = jnp.sum(column_terms, axis=0, keepdims=True)
    for j in range(4):
        for b in range(2):
            for k in range(width // 128):
                small_send[j, b, k : k + 1, :] = columns[:, k * 128 : (k + 1) * 128]
    me = x * 4 + z
    small_recv[me] = small_send[0, x]
    small = [
        send(
            small_send.at[slot[0], slot[1]],
            small_recv.at[me],
            sm_send.at[k],
            sm_recv.at[k],
            peers[k],
        )
        for k, slot in enumerate(small_slots)
    ]
    add_across(3)
    for copy in small:
        copy.wait_recv()
    total = small_recv[0]
    for k in range(1, 8):
        total = total + small_recv[k]
    col_ref[...] = total[0:8] / math.sqrt(total_tokens)
    row_ref[...] = total[8:16] / math.sqrt(model_width)
    for j in range(1, 4):
        mz[j].wait_recv()
    mixed_ref[...] = (
        own_sum[...]
        + z_recv[0].astype(jnp.float32)
        + z_recv[1].astype(jnp.float32)
        + z_recv[2].astype(jnp.float32)
    ).astype(jnp.bfloat16)
    for copy in sent:
        copy.wait_send()


def per_device_kernel(tokens, gate_up, down_weight):
    block, width = tokens.shape
    units = down_weight.shape[0]
    half = units // 2
    total_tokens = block * lax.axis_size(("dp", "col"))
    model_width = width * lax.axis_size("row")
    dma = pltpu.SemaphoreType.DMA
    bf16, f32 = jnp.bfloat16, jnp.float32
    sems = []
    for count in (2, 3, 4, 8, 4, 4, 4, 4, 4, 3, 3, 7):
        sems += [dma((count,)), dma((count,))]
    mixed, col, row = pl.pallas_call(
        functools.partial(kernel, total_tokens, model_width),
        out_shape=(
            jax.ShapeDtypeStruct((block, width), bf16),
            jax.ShapeDtypeStruct((8, 128), f32),
            jax.ShapeDtypeStruct((8, 128), f32),
        ),
        in_specs=[pl.BlockSpec(memory_space=pl.ANY)] * 3,
        out_specs=(pl.BlockSpec(memory_space=pltpu.VMEM),) * 3,
        scratch_shapes=[
            pltpu.VMEM((2, width, units), bf16),
            pltpu.VMEM((units, width), bf16),
            pltpu.VMEM((4, 2, 2, block, width), bf16),
            pltpu.VMEM((4, 2, block, units), f32),
            pltpu.VMEM((4, 2, block, units), bf16),
            pltpu.VMEM((4, block, units), bf16),
            pltpu.VMEM((4, 2, 2, block, half), bf16),
            pltpu.VMEM((4, 2, block, width), f32),
            pltpu.VMEM((4, 2, block, width), bf16),
            pltpu.VMEM((4, block, width), bf16),
            pltpu.VMEM((3, block, width), bf16),
            pltpu.VMEM((3, block, width), bf16),
            pltpu.VMEM((block, width), f32),
            pltpu.VMEM((2, 8, half), f32),
            pltpu.VMEM((4, 2, 8, half), f32),
            pltpu.VMEM((2, 8, half), bf16),
            pltpu.VMEM((4, 2, 16, 128), f32),
            pltpu.VMEM((8, 16, 128), f32),
            dma((4,)),
        ]
        + sems,
        compiler_params=pltpu.CompilerParams(
            collective_id=0, has_side_effects=True, vmem_limit_bytes=56 * 2**20
        ),
        name="swiglu_grid",
    )(tokens, gate_up, down_weight)
    return mixed, col.reshape(width), row[0, :block]


def fits_kernel(mesh):
    return dict(mesh.shape) == {"dp": 2, "row": 4, "col": 4}


def solution(mesh):
    body = per_device_kernel if fits_kernel(mesh) else per_device
    placed = (P(("dp", "col"), "row"), P(None, "row", ("dp", "col")), P(("dp", "col"), "row"))
    return jax.shard_map(
        body,
        mesh=mesh,
        in_specs=placed,
        out_specs=(P(("dp", "col"), "row"), P("row"), P(("dp", "col"))),
        check_vma=False,
    )
```

```python
import functools
import math

import jax
import jax.numpy as jnp
from jax import lax
from jax.experimental import pallas as pl
from jax.experimental.pallas import tpu as pltpu
from jax.sharding import PartitionSpec as P

MESH = pl.DeviceIdType.MESH
TILE = 256


def swiglu(partial_value):
    return (jax.nn.silu(partial_value[:, 0]) * partial_value[:, 1]).astype(jnp.bfloat16)


def hidden_units(partial_value):
    share = lax.psum_scatter(partial_value, "row", scatter_dimension=0, tiled=True)
    return lax.all_gather(swiglu(share), "row", axis=0, tiled=True)


def make_accumulate(hidden, shard_piece):
    columns_wide = hidden.astype(jnp.float32)
    piece_wide = shard_piece.astype(jnp.float32)
    output_part = jnp.dot(hidden, shard_piece, preferred_element_type=jnp.float32)
    column_part = jnp.dot(
        jnp.sum(columns_wide, axis=0), piece_wide, precision=lax.Precision.HIGHEST
    )
    row_part = jnp.dot(columns_wide, jnp.sum(piece_wide, axis=1), precision=lax.Precision.HIGHEST)
    return (output_part, column_part, row_part)


def per_device(tokens, gate_up, down_weight):
    total_tokens = tokens.shape[0] * lax.axis_size(("dp", "col"))
    model_width = tokens.shape[1] * lax.axis_size("row")
    group_rows = lax.all_gather(tokens, "col", axis=0, tiled=True)
    partial_value = jnp.einsum(
        "td,gdf->tgf",
        group_rows,
        lax.all_gather(gate_up, "dp", axis=2, tiled=True),
        preferred_element_type=jnp.float32,
    )
    hidden = hidden_units(partial_value)
    output_part, column_part, row_part = make_accumulate(
        hidden, lax.all_gather(down_weight, "dp", axis=0, tiled=True)
    )
    mixed, row_share = (
        lax.psum_scatter(output_part, "col", scatter_dimension=0, tiled=True),
        lax.psum_scatter(row_part, "col", scatter_dimension=0, tiled=True),
    )
    col_check = lax.psum(column_part, ("dp", "col")) / math.sqrt(total_tokens)
    row_check = lax.psum(row_share, "row") / math.sqrt(model_width)
    return (mixed.astype(jnp.bfloat16), col_check, row_check)


def dot(a, b):
    return jnp.dot(a, b, preferred_element_type=jnp.float32)


def dot_rows(a, b):
    return lax.dot_general(a, b, (((1,), (1,)), ((), ())), preferred_element_type=jnp.float32)


def three_terms(row):
    high = row.astype(jnp.bfloat16)
    rest = row - high.astype(jnp.float32)
    middle = rest.astype(jnp.bfloat16)
    low = (rest - middle.astype(jnp.float32)).astype(jnp.bfloat16)
    index = lax.broadcasted_iota(jnp.int32, row.shape, 0)
    terms = jnp.where(
        index == 0,
        high.astype(jnp.float32),
        jnp.where(
            index == 1,
            middle.astype(jnp.float32),
            jnp.where(index == 2, low.astype(jnp.float32), 0.0),
        ),
    )
    return terms.astype(jnp.bfloat16)


def kernel(
    total_tokens,
    model_width,
    tokens_ref,
    gate_up_ref,
    down_ref,
    mixed_ref,
    col_ref,
    row_ref,
    weights,
    down,
    acts,
    part_wide,
    part_send,
    part_recv,
    hidden,
    out_wide,
    out_send,
    x_recv,
    z_send,
    z_recv,
    own_sum,
    unit_sums,
    weight_parts,
    weight_terms,
    small_send,
    small_recv,
    local_sem,
    w_send,
    w_recv,
    tz_send,
    tz_recv,
    tx_send,
    tx_recv,
    tp_send,
    tp_recv,
    py_send,
    py_recv,
    hp_send,
    hp_recv,
    hy_send,
    hy_recv,
    hf_send,
    hf_recv,
    mx_send,
    mx_recv,
    mz_send,
    mz_recv,
    ws_send,
    ws_recv,
    sm_send,
    sm_recv,
):
    block, width = tokens_ref.shape
    units = down_ref.shape[0]
    half = units // 2
    first = (half // 128 + 1) // 2 * 128
    pieces = [(0, first, 0), (first, half - first, 2 * first)]
    strip = width // 2
    x = lax.axis_index("dp")
    row = lax.axis_index("row")
    z = lax.axis_index("col")
    y, core = lax.div(row, 2), lax.rem(row, 2)
    nx, ny, ncore = 1 - x, 1 - y, 1 - core
    zs = [z, lax.rem(z + 2, 4), 3 - z, z + 1 - 2 * lax.rem(z, 2)]
    partner = (x, y * 2 + ncore, z)
    across_y = (x, ny * 2 + core, z)
    across_x = (nx, row, z)
    rows = [(x, lax.rem(row + k, 4), z) for k in range(1, 4)]
    peers = [(x, row, zs[j]) for j in range(1, 4)] + [(nx, row, zs[j]) for j in range(4)]
    small_slots = [(j, x) for j in range(1, 4)] + [(j, nx) for j in range(4)]
    sent = []

    def send(src, dst, send_sem, recv_sem, device):
        copy = pltpu.make_async_remote_copy(
            src_ref=src,
            dst_ref=dst,
            send_sem=send_sem,
            recv_sem=recv_sem,
            device_id=device,
            device_id_type=MESH,
        )
        copy.start()
        sent.append(copy)
        return copy

    def weight_slices(which):
        for start, count, column in pieces:
            lanes = pl.ds(pl.multiple_of(which * half + start, 128), count)
            for g in range(2):
                place = slice(column + g * count, column + (g + 1) * count)
                yield gate_up_ref.at[g, :, lanes], weights.at[core, :, place]

    local = [pltpu.make_async_copy(tokens_ref, acts.at[z, core, x], local_sem.at[0])]
    for k, (src, dst) in enumerate(weight_slices(core)):
        local.append(pltpu.make_async_copy(src, dst, local_sem.at[1 + k]))
    local.append(pltpu.make_async_copy(down_ref, down, local_sem.at[5]))
    for copy in local:
        copy.start()

    barrier = pltpu.get_barrier_semaphore()
    for device in rows + peers:
        pl.semaphore_signal(barrier, inc=1, device_id=device, device_id_type=MESH)
    pl.semaphore_wait(barrier, len(rows) + len(peers))

    tx, tp, tz = {}, {}, {}
    tx[0] = send(tokens_ref, acts.at[z, core, x], tx_send.at[0], tx_recv.at[0], across_x)
    tp[0, 0] = send(tokens_ref, acts.at[z, core, x], tp_send.at[0], tp_recv.at[0], partner)

    def offer(j):
        tz[j] = send(
            tokens_ref, acts.at[z, core, x], tz_send.at[j - 1], tz_recv.at[j - 1], peers[j - 1]
        )

    offer(1)
    swap = [
        send(src, dst, w_send.at[k], w_recv.at[k], partner)
        for k, (src, dst) in enumerate(weight_slices(ncore))
    ]

    unit_sums[...] = jnp.zeros_like(unit_sums)
    small_send[...] = jnp.zeros_like(small_send)

    weight_copies = []

    def sum_weights():
        local[5].wait()
        ones_width = jnp.ones((8, width), jnp.bfloat16)
        for h in range(2):
            weight_parts[row, h] = dot_rows(ones_width, down[h * half : (h + 1) * half, :])
        place = weight_parts.at[row]
        for k in range(3):
            weight_copies.append(send(place, place, ws_send.at[k], ws_recv.at[k], rows[k]))

    def total_weights():
        for copy in weight_copies:
            copy.wait_recv()
        for h in range(2):
            weight_terms[h] = three_terms(
                weight_parts[0, h] + weight_parts[1, h] + weight_parts[2, h] + weight_parts[3, h]
            )

    def arrive(j):
        tz[j].wait_recv()
        place = acts.at[zs[j], core, x]
        tx[j] = send(place, place, tx_send.at[j], tx_recv.at[j], across_x)
        tp[j, 0] = send(place, place, tp_send.at[2 * j], tp_recv.at[2 * j], partner)

    def arrive_across(j):
        tx[j].wait_recv()
        place = acts.at[zs[j], core, nx]
        tp[j, 1] = send(place, place, tp_send.at[2 * j + 1], tp_recv.at[2 * j + 1], partner)

    py, hp, hy, hf, mx, mz = {}, {}, {}, {}, {}, {}

    def ready(j):
        tp[j, 0].wait_recv()
        tp[j, 1].wait_recv()

    def gate_and_up(j, p):
        _, count, column = pieces[p]

        def body(t, carry):
            columns = pl.ds(pl.multiple_of(t * TILE, TILE), TILE)
            product = dot(
                acts[zs[j], 0].reshape(2 * block, width), weights[0, :, columns]
            ) + dot(acts[zs[j], 1].reshape(2 * block, width), weights[1, :, columns])
            product = product.reshape(2, block, TILE)
            part_wide[j, :, :, columns] = product
            part_send[j, :, :, columns] = product.astype(jnp.bfloat16)
            return carry

        lax.fori_loop(column // TILE, (column + 2 * count) // TILE, body, 0)
        place = slice(column, column + 2 * count)
        py[j, p] = send(
            part_send.at[j, ny, :, place],
            part_recv.at[j, :, place],
            py_send.at[2 * j + p],
            py_recv.at[2 * j + p],
            across_y,
        )

    def activate(j, p):
        start, count, column = pieces[p]
        py[j, p].wait_recv()
        gate, up = [
            part_wide[j, y, :, place] + part_recv[j, :, place].astype(jnp.float32)
            for place in (
                slice(column, column + count),
                slice(column + count, column + 2 * count),
            )
        ]
        lanes = slice(start, start + count)
        hidden[j, core, y, :, lanes] = (gate / (1.0 + jnp.exp(-gate)) * up).astype(jnp.bfloat16)
        place = hidden.at[j, core, y, :, lanes]
        n = 2 * j + p
        hy[j, p] = send(place, place, hy_send.at[n], hy_recv.at[n], across_y)
        hp[j, p] = send(place, place, hp_send.at[n], hp_recv.at[n], partner)

    def hand_over(j, p):
        start, count, _ = pieces[p]
        hy[j, p].wait_recv()
        place = hidden.at[j, core, ny, :, start : start + count]
        n = 2 * j + p
        hf[j, p] = send(place, place, hf_send.at[n], hf_recv.at[n], partner)

    def down_part(j):
        for p in range(2):
            hp[j, p].wait_recv()
            hf[j, p].wait_recv()

        def body(t, carry):
            columns = pl.ds(pl.multiple_of(t * TILE, TILE), TILE)
            product = dot(
                hidden[j, 0].reshape(2 * block, half), down[0:half, columns]
            ) + dot(hidden[j, 1].reshape(2 * block, half), down[half:units, columns])
            product = product.reshape(2, block, TILE)
            out_wide[j, :, :, columns] = product
            out_send[j, :, :, columns] = product.astype(jnp.bfloat16)
            return carry

        for q in range(2):
            lax.fori_loop(q * strip // TILE, (q + 1) * strip // TILE, body, 0)
            place = slice(q * strip, (q + 1) * strip)
            n = 2 * j + q
            mx[j, q] = send(
                out_send.at[j, nx, :, place],
                x_recv.at[j, :, place],
                mx_send.at[n],
                mx_recv.at[n],
                across_x,
            )

    def checks(j):
        ones = jnp.ones((8, 2 * block), jnp.bfloat16)
        for h in range(2):
            unit_sums[h] += dot(ones, hidden[j, h].reshape(2 * block, half))
        for b in range(2):
            terms = dot_rows(weight_terms[0], hidden[j, 0, b]) + dot_rows(
                weight_terms[1], hidden[j, 1, b]
            )
            small_send[j, b, 8:9, 0:block] = jnp.sum(terms, axis=0, keepdims=True)

    def add_across(j):
        for q in range(2):
            mx[j, q].wait_recv()
            place = slice(q * strip, (q + 1) * strip)
            value = out_wide[j, x, :, place] + x_recv[j, :, place].astype(jnp.float32)
            if j == 0:
                own_sum[:, place] = value
            else:
                z_send[j - 1, :, place] = value.astype(jnp.bfloat16)
                n = 2 * (j - 1) + q
                mz[j, q] = send(
                    z_send.at[j - 1, :, place],
                    z_recv.at[j - 1, :, place],
                    mz_send.at[n],
                    mz_recv.at[n],
                    peers[j - 1],
                )

    def weights_here(p):
        for k in (2 * p, 2 * p + 1):
            local[1 + k].wait()
            swap[k].wait_recv()

    local[0].wait()
    arrive_across(0)
    weights_here(0)
    ready(0)
    gate_and_up(0, 0)
    weights_here(1)
    gate_and_up(0, 1)
    arrive(1)
    offer(2)
    sum_weights()
    activate(0, 0)
    arrive_across(1)
    ready(1)
    gate_and_up(1, 0)
    gate_and_up(1, 1)
    arrive(2)
    offer(3)
    activate(0, 1)
    hand_over(0, 0)
    total_weights()
    arrive_across(2)
    ready(2)
    gate_and_up(2, 0)
    gate_and_up(2, 1)
    arrive(3)
    activate(1, 0)
    hand_over(0, 1)
    activate(1, 1)
    arrive_across(3)
    ready(3)
    gate_and_up(3, 0)
    gate_and_up(3, 1)
    hand_over(1, 0)
    down_part(0)
    activate(2, 0)
    hand_over(1, 1)
    activate(2, 1)
    down_part(1)
    add_across(0)
    checks(0)
    hand_over(2, 0)
    activate(3, 0)
    hand_over(2, 1)
    activate(3, 1)
    add_across(1)
    down_part(2)
    checks(1)
    checks(2)
    add_across(2)
    hand_over(3, 0)
    hand_over(3, 1)
    down_part(3)
    checks(3)

    column_terms = dot(three_terms(unit_sums[0]), down[0:half, :]) + dot(
        three_terms(unit_sums[1]), down[half:units, :]
    )
    columns = jnp.sum(column_terms, axis=0, keepdims=True)
    for j in range(4):
        for b in range(2):
            for k in range(width // 128):
                small_send[j, b, k : k + 1, :] = columns[:, k * 128 : (k + 1) * 128]
    me = x * 4 + z
    small_recv[me] = small_send[0, x]
    small = [
        send(
            small_send.at[slot[0], slot[1]],
            small_recv.at[me],
            sm_send.at[k],
            sm_recv.at[k],
            peers[k],
        )
        for k, slot in enumerate(small_slots)
    ]
    add_across(3)
    for copy in small:
        copy.wait_recv()
    total = small_recv[0]
    for k in range(1, 8):
        total = total + small_recv[k]
    col_ref[...] = total[0:8] / math.sqrt(total_tokens)
    row_ref[...] = total[8:16] / math.sqrt(model_width)
    for q in range(2):
        place = slice(q * strip, (q + 1) * strip)
        value = own_sum[:, place]
        for j in range(1, 4):
            mz[j, q].wait_recv()
            value = value + z_recv[j - 1, :, place].astype(jnp.float32)
        mixed_ref[:, place] = value.astype(jnp.bfloat16)
    for copy in sent:
        copy.wait_send()


def per_device_kernel(tokens, gate_up, down_weight):
    block, width = tokens.shape
    units = down_weight.shape[0]
    half = units // 2
    total_tokens = block * lax.axis_size(("dp", "col"))
    model_width = width * lax.axis_size("row")
    dma = pltpu.SemaphoreType.DMA
    bf16, f32 = jnp.bfloat16, jnp.float32
    sems = []
    for count in (4, 3, 4, 8, 8, 8, 8, 8, 8, 6, 3, 7):
        sems += [dma((count,)), dma((count,))]
    mixed, col, row = pl.pallas_call(
        functools.partial(kernel, total_tokens, model_width),
        out_shape=(
            jax.ShapeDtypeStruct((block, width), bf16),
            jax.ShapeDtypeStruct((8, 128), f32),
            jax.ShapeDtypeStruct((8, 128), f32),
        ),
        in_specs=[pl.BlockSpec(memory_space=pl.ANY)] * 3,
        out_specs=(pl.BlockSpec(memory_space=pltpu.VMEM),) * 3,
        scratch_shapes=[
            pltpu.VMEM((2, width, units), bf16),
            pltpu.VMEM((units, width), bf16),
            pltpu.VMEM((4, 2, 2, block, width), bf16),
            pltpu.VMEM((4, 2, block, units), f32),
            pltpu.VMEM((4, 2, block, units), bf16),
            pltpu.VMEM((4, block, units), bf16),
            pltpu.VMEM((4, 2, 2, block, half), bf16),
            pltpu.VMEM((4, 2, block, width), f32),
            pltpu.VMEM((4, 2, block, width), bf16),
            pltpu.VMEM((4, block, width), bf16),
            pltpu.VMEM((3, block, width), bf16),
            pltpu.VMEM((3, block, width), bf16),
            pltpu.VMEM((block, width), f32),
            pltpu.VMEM((2, 8, half), f32),
            pltpu.VMEM((4, 2, 8, half), f32),
            pltpu.VMEM((2, 8, half), bf16),
            pltpu.VMEM((4, 2, 16, 128), f32),
            pltpu.VMEM((8, 16, 128), f32),
            dma((6,)),
        ]
        + sems,
        compiler_params=pltpu.CompilerParams(
            collective_id=0, has_side_effects=True, vmem_limit_bytes=56 * 2**20
        ),
        name="swiglu_grid",
    )(tokens, gate_up, down_weight)
    return mixed, col.reshape(width), row[0, :block]


def fits_kernel(mesh):
    return dict(mesh.shape) == {"dp": 2, "row": 4, "col": 4}


def solution(mesh):
    body = per_device_kernel if fits_kernel(mesh) else per_device
    placed = (P(("dp", "col"), "row"), P(None, "row", ("dp", "col")), P(("dp", "col"), "row"))
    return jax.shard_map(
        body,
        mesh=mesh,
        in_specs=placed,
        out_specs=(P(("dp", "col"), "row"), P("row"), P(("dp", "col"))),
        check_vma=False,
    )
```

```python
import functools
import math

import jax
import jax.numpy as jnp
from jax import lax
from jax.experimental import pallas as pl
from jax.experimental.pallas import tpu as pltpu
from jax.sharding import PartitionSpec as P

MESH = pl.DeviceIdType.MESH
TILE = 256


def swiglu(partial_value):
    return (jax.nn.silu(partial_value[:, 0]) * partial_value[:, 1]).astype(jnp.bfloat16)


def hidden_units(partial_value):
    share = lax.psum_scatter(partial_value, "row", scatter_dimension=0, tiled=True)
    return lax.all_gather(swiglu(share), "row", axis=0, tiled=True)


def make_accumulate(hidden, shard_piece):
    columns_wide = hidden.astype(jnp.float32)
    piece_wide = shard_piece.astype(jnp.float32)
    output_part = jnp.dot(hidden, shard_piece, preferred_element_type=jnp.float32)
    column_part = jnp.dot(
        jnp.sum(columns_wide, axis=0), piece_wide, precision=lax.Precision.HIGHEST
    )
    row_part = jnp.dot(columns_wide, jnp.sum(piece_wide, axis=1), precision=lax.Precision.HIGHEST)
    return (output_part, column_part, row_part)


def per_device(tokens, gate_up, down_weight):
    total_tokens = tokens.shape[0] * lax.axis_size(("dp", "col"))
    model_width = tokens.shape[1] * lax.axis_size("row")
    group_rows = lax.all_gather(tokens, "col", axis=0, tiled=True)
    partial_value = jnp.einsum(
        "td,gdf->tgf",
        group_rows,
        lax.all_gather(gate_up, "dp", axis=2, tiled=True),
        preferred_element_type=jnp.float32,
    )
    hidden = hidden_units(partial_value)
    output_part, column_part, row_part = make_accumulate(
        hidden, lax.all_gather(down_weight, "dp", axis=0, tiled=True)
    )
    mixed, row_share = (
        lax.psum_scatter(output_part, "col", scatter_dimension=0, tiled=True),
        lax.psum_scatter(row_part, "col", scatter_dimension=0, tiled=True),
    )
    col_check = lax.psum(column_part, ("dp", "col")) / math.sqrt(total_tokens)
    row_check = lax.psum(row_share, "row") / math.sqrt(model_width)
    return (mixed.astype(jnp.bfloat16), col_check, row_check)


def dot(a, b):
    return jnp.dot(a, b, preferred_element_type=jnp.float32)


def dot_rows(a, b):
    return lax.dot_general(a, b, (((1,), (1,)), ((), ())), preferred_element_type=jnp.float32)


def three_terms(row):
    high = row.astype(jnp.bfloat16)
    rest = row - high.astype(jnp.float32)
    middle = rest.astype(jnp.bfloat16)
    low = (rest - middle.astype(jnp.float32)).astype(jnp.bfloat16)
    index = lax.broadcasted_iota(jnp.int32, row.shape, 0)
    terms = jnp.where(
        index == 0,
        high.astype(jnp.float32),
        jnp.where(
            index == 1,
            middle.astype(jnp.float32),
            jnp.where(index == 2, low.astype(jnp.float32), 0.0),
        ),
    )
    return terms.astype(jnp.bfloat16)


def kernel(
    total_tokens,
    model_width,
    tokens_ref,
    gate_up_ref,
    down_ref,
    mixed_ref,
    col_ref,
    row_ref,
    weights,
    down,
    acts,
    part_wide,
    part_send,
    part_recv,
    hidden,
    out_wide,
    out_send,
    x_recv,
    z_send,
    z_recv,
    own_sum,
    unit_sums,
    weight_parts,
    weight_terms,
    small_send,
    small_recv,
    local_sem,
    w_send,
    w_recv,
    tz_send,
    tz_recv,
    tx_send,
    tx_recv,
    tp_send,
    tp_recv,
    py_send,
    py_recv,
    hp_send,
    hp_recv,
    hy_send,
    hy_recv,
    hf_send,
    hf_recv,
    mx_send,
    mx_recv,
    mz_send,
    mz_recv,
    ws_send,
    ws_recv,
    sm_send,
    sm_recv,
):
    block, width = tokens_ref.shape
    units = down_ref.shape[0]
    half = units // 2
    group = half // 256 * 128
    left = half - 2 * group
    wide, last = 2 * group, 4 * group
    strip = width // 2
    x = lax.axis_index("dp")
    row = lax.axis_index("row")
    z = lax.axis_index("col")
    y, core = lax.div(row, 2), lax.rem(row, 2)
    nx, ny, ncore = 1 - x, 1 - y, 1 - core
    zs = [z, z + 1 - 2 * lax.rem(z, 2), lax.rem(z + 2, 4), 3 - z]
    partner = (x, y * 2 + ncore, z)
    across_y = (x, ny * 2 + core, z)
    across_x = (nx, row, z)
    rows = [(x, lax.rem(row + k, 4), z) for k in range(1, 4)]
    peers = [(x, row, zs[j]) for j in range(1, 4)] + [(nx, row, zs[j]) for j in range(4)]
    small_slots = [(j, x) for j in range(1, 4)] + [(j, nx) for j in range(4)]
    sent = []

    def send(src, dst, send_sem, recv_sem, device):
        copy = pltpu.make_async_remote_copy(
            src_ref=src,
            dst_ref=dst,
            send_sem=send_sem,
            recv_sem=recv_sem,
            device_id=device,
            device_id_type=MESH,
        )
        copy.start()
        sent.append(copy)
        return copy

    def weight_slices(which):
        for start, count in ((ny * group, group), (2 * group, left), (y * group, group)):
            for g in range(2):
                lanes = pl.ds(pl.multiple_of(which * half + start, 128), count)
                place = pl.ds(pl.multiple_of(2 * start + g * count, 128), count)
                yield gate_up_ref.at[g, :, lanes], weights.at[core, :, place]

    local = [pltpu.make_async_copy(tokens_ref, acts.at[z, core, x], local_sem.at[0])]
    for k, (src, dst) in enumerate(weight_slices(core)):
        local.append(pltpu.make_async_copy(src, dst, local_sem.at[1 + k]))
    local.append(pltpu.make_async_copy(down_ref, down, local_sem.at[7]))
    for copy in local:
        copy.start()

    barrier = pltpu.get_barrier_semaphore()
    for device in rows + peers:
        pl.semaphore_signal(barrier, inc=1, device_id=device, device_id_type=MESH)
    pl.semaphore_wait(barrier, len(rows) + len(peers))

    tx, tp, tz = {}, {}, {}
    tx[0] = send(tokens_ref, acts.at[z, core, x], tx_send.at[0], tx_recv.at[0], across_x)
    tp[0, 0] = send(tokens_ref, acts.at[z, core, x], tp_send.at[0], tp_recv.at[0], partner)

    def offer(j):
        tz[j] = send(
            tokens_ref, acts.at[z, core, x], tz_send.at[j - 1], tz_recv.at[j - 1], peers[j - 1]
        )

    offer(1)
    swap = [
        send(src, dst, w_send.at[k], w_recv.at[k], partner)
        for k, (src, dst) in enumerate(weight_slices(ncore))
    ]

    unit_sums[...] = jnp.zeros_like(unit_sums)
    small_send[...] = jnp.zeros_like(small_send)

    weight_copies = []

    def sum_weights():
        local[7].wait()
        ones_width = jnp.ones((8, width), jnp.bfloat16)
        for h in range(2):
            weight_parts[row, h] = dot_rows(ones_width, down[h * half : (h + 1) * half, :])
        place = weight_parts.at[row]
        for k in range(3):
            weight_copies.append(send(place, place, ws_send.at[k], ws_recv.at[k], rows[k]))

    def total_weights():
        for copy in weight_copies:
            copy.wait_recv()
        for h in range(2):
            weight_terms[h] = three_terms(
                weight_parts[0, h] + weight_parts[1, h] + weight_parts[2, h] + weight_parts[3, h]
            )

    def arrive(j):
        tz[j].wait_recv()
        place = acts.at[zs[j], core, x]
        tx[j] = send(place, place, tx_send.at[j], tx_recv.at[j], across_x)
        tp[j, 0] = send(place, place, tp_send.at[2 * j], tp_recv.at[2 * j], partner)

    def arrive_across(j):
        tx[j].wait_recv()
        place = acts.at[zs[j], core, nx]
        tp[j, 1] = send(place, place, tp_send.at[2 * j + 1], tp_recv.at[2 * j + 1], partner)

    py, hp, hy, hf, mx, mz = {}, {}, {}, {}, {}, {}

    def ready(j):
        tp[j, 0].wait_recv()
        tp[j, 1].wait_recv()

    def columns_of(tile):
        return pl.ds(pl.multiple_of(tile * TILE, TILE), TILE)

    def multiply_block(b, tile, tiles):
        def body(t, carry):
            columns = columns_of(tile + t)
            product = dot(acts[z, 0, b], weights[0, :, columns]) + dot(
                acts[z, 1, b], weights[1, :, columns]
            )
            part_send[0, b, :, columns] = product.astype(jnp.bfloat16)
            return carry

        lax.fori_loop(0, tiles, body, 0)

    def multiply(j, tile, tiles):
        def body(t, carry):
            columns = columns_of(tile + t)
            product = dot(
                acts[zs[j], 0].reshape(2 * block, width), weights[0, :, columns]
            ) + dot(acts[zs[j], 1].reshape(2 * block, width), weights[1, :, columns])
            product = product.reshape(2, block, TILE)
            part_wide[j, :, :, columns] = product
            part_send[j, :, :, columns] = product.astype(jnp.bfloat16)
            return carry

        lax.fori_loop(0, tiles, body, 0)

    def send_part(n, j, b, place):
        py[n] = send(
            part_send.at[j, b, :, place],
            part_recv.at[j, b, :, place],
            py_send.at[n],
            py_recv.at[n],
            across_y,
        )

    def at_128(start, count):
        return pl.ds(pl.multiple_of(start, 128), count)

    def terms_of(n):
        if n < 2:
            return 0, [((x, nx)[n], y * wide, group, y * group)]
        if n == 2:
            return 0, [(y, last, left, wide)]
        j, p = divmod(n - 1, 2)
        if p == 0:
            return j, [(y, 0, group, 0)]
        return j, [(y, wide, group, group), (y, last, left, wide)]

    def hidden_place(n, who):
        if n < 2:
            return hidden.at[0, core, (x, nx)[n], :, at_128(who * group, group)]
        if n == 2:
            return hidden.at[0, core, who, :, wide:half]
        j, p = divmod(n - 1, 2)
        lanes = slice(0, group) if p == 0 else slice(group, half)
        return hidden.at[j, core, who, :, lanes]

    def activate(n):
        py[n].wait_recv()
        j, terms = terms_of(n)
        for b, column, count, unit in terms:
            gate, up = [
                part_wide[j, b, :, place] + part_recv[j, b, :, place].astype(jnp.float32)
                for place in (at_128(column, count), at_128(column + count, count))
            ]
            value = gate / (1.0 + jnp.exp(-gate)) * up
            hidden[j, core, b, :, at_128(unit, count)] = value.astype(jnp.bfloat16)
        place = hidden_place(n, y)
        hp[n] = send(place, place, hp_send.at[n], hp_recv.at[n], partner)

    def across(n):
        place = hidden_place(n, y)
        hy[n] = send(place, place, hy_send.at[n], hy_recv.at[n], across_y)

    def hand_over(n):
        hy[n].wait_recv()
        place = hidden_place(n, ny)
        hf[n] = send(place, place, hf_send.at[n], hf_recv.at[n], partner)

    def gate_and_up(j):
        ready(j)
        multiply(j, 0, wide // TILE)
        send_part(1 + 2 * j, j, ny, slice(0, wide))
        multiply(j, wide // TILE, (units - wide) // TILE)
        send_part(2 + 2 * j, j, ny, slice(wide, units))

    def down_part(j):
        for n in (0, 1, 2) if j == 0 else (1 + 2 * j, 2 + 2 * j):
            hp[n].wait_recv()
            hf[n].wait_recv()

        def body(t, carry):
            columns = columns_of(t)
            product = dot(
                hidden[j, 0].reshape(2 * block, half), down[0:half, columns]
            ) + dot(hidden[j, 1].reshape(2 * block, half), down[half:units, columns])
            product = product.reshape(2, block, TILE)
            out_wide[j, :, :, columns] = product
            out_send[j, :, :, columns] = product.astype(jnp.bfloat16)
            return carry

        for q in range(2):
            lax.fori_loop(q * strip // TILE, (q + 1) * strip // TILE, body, 0)
            place = slice(q * strip, (q + 1) * strip)
            n = 2 * j + q
            mx[j, q] = send(
                out_send.at[j, nx, :, place],
                x_recv.at[j, :, place],
                mx_send.at[n],
                mx_recv.at[n],
                across_x,
            )

    def checks(j):
        ones = jnp.ones((8, 2 * block), jnp.bfloat16)
        for h in range(2):
            unit_sums[h] += dot(ones, hidden[j, h].reshape(2 * block, half))
        for b in range(2):
            terms = dot_rows(weight_terms[0], hidden[j, 0, b]) + dot_rows(
                weight_terms[1], hidden[j, 1, b]
            )
            small_send[j, b, 8:9, 0:block] = jnp.sum(terms, axis=0, keepdims=True)

    def add_across(j):
        for q in range(2):
            mx[j, q].wait_recv()
            place = slice(q * strip, (q + 1) * strip)
            value = out_wide[j, x, :, place] + x_recv[j, :, place].astype(jnp.float32)
            if j == 0:
                own_sum[:, place] = value
            else:
                z_send[j - 1, :, place] = value.astype(jnp.bfloat16)
                n = 2 * (j - 1) + q
                mz[j, q] = send(
                    z_send.at[j - 1, :, place],
                    z_recv.at[j - 1, :, place],
                    mz_send.at[n],
                    mz_recv.at[n],
                    peers[j - 1],
                )

    def weights_here(p):
        for k in (2 * p, 2 * p + 1):
            local[1 + k].wait()
            swap[k].wait_recv()

    local[0].wait()
    tp[0, 0].wait_recv()
    weights_here(0)
    multiply_block(x, ny * (wide // TILE), wide // TILE)
    send_part(0, 0, x, at_128(ny * wide, wide))
    offer(2)
    arrive_across(0)
    arrive(1)
    tp[0, 1].wait_recv()
    multiply_block(nx, ny * (wide // TILE), wide // TILE)
    send_part(1, 0, nx, at_128(ny * wide, wide))
    weights_here(1)
    multiply(0, last // TILE, 2 * left // TILE)
    send_part(2, 0, ny, slice(last, units))
    weights_here(2)
    multiply(0, y * (wide // TILE), wide // TILE)
    sum_weights()
    activate(0)
    across(0)
    activate(1)
    arrive_across(1)
    gate_and_up(1)
    activate(2)
    arrive(2)
    offer(3)
    total_weights()
    hand_over(0)
    activate(3)
    arrive_across(2)
    gate_and_up(2)
    activate(4)
    arrive(3)
    activate(5)
    across(5)
    activate(6)
    across(6)
    arrive_across(3)
    gate_and_up(3)
    across(3)
    hand_over(5)
    hand_over(6)
    down_part(2)
    activate(7)
    across(7)
    activate(8)
    across(8)
    across(4)
    across(1)
    across(2)
    add_across(2)
    checks(2)
    hand_over(3)
    hand_over(7)
    hand_over(8)
    down_part(3)
    hand_over(4)
    down_part(1)
    add_across(3)
    checks(3)
    checks(1)
    hand_over(1)
    hand_over(2)
    down_part(0)
    add_across(1)
    checks(0)

    column_terms = dot(three_terms(unit_sums[0]), down[0:half, :]) + dot(
        three_terms(unit_sums[1]), down[half:units, :]
    )
    columns = jnp.sum(column_terms, axis=0, keepdims=True)
    for j in range(4):
        for b in range(2):
            for k in range(width // 128):
                small_send[j, b, k : k + 1, :] = columns[:, k * 128 : (k + 1) * 128]
    me = x * 4 + z
    small_recv[me] = small_send[0, x]
    small = [
        send(
            small_send.at[slot[0], slot[1]],
            small_recv.at[me],
            sm_send.at[k],
            sm_recv.at[k],
            peers[k],
        )
        for k, slot in enumerate(small_slots)
    ]
    add_across(0)
    for copy in small:
        copy.wait_recv()
    total = small_recv[0]
    for k in range(1, 8):
        total = total + small_recv[k]
    col_ref[...] = total[0:8] / math.sqrt(total_tokens)
    row_ref[...] = total[8:16] / math.sqrt(model_width)
    for q in range(2):
        place = slice(q * strip, (q + 1) * strip)
        value = own_sum[:, place]
        for j in range(1, 4):
            mz[j, q].wait_recv()
            value = value + z_recv[j - 1, :, place].astype(jnp.float32)
        mixed_ref[:, place] = value.astype(jnp.bfloat16)
    for copy in sent:
        copy.wait_send()


def write_results(mixed_ref, col_ref, row_ref, mixed_out, col_out, row_out):
    mixed_out[...] = mixed_ref[...]
    for k in range(col_ref.shape[0]):
        col_out[pl.ds(k * 128, 128)] = col_ref[k]
    row_out[...] = row_ref[0, 0 : row_out.shape[0]]


def per_device_kernel(tokens, gate_up, down_weight):
    block, width = tokens.shape
    units = down_weight.shape[0]
    half = units // 2
    total_tokens = block * lax.axis_size(("dp", "col"))
    model_width = width * lax.axis_size("row")
    dma = pltpu.SemaphoreType.DMA
    bf16, f32 = jnp.bfloat16, jnp.float32
    sems = []
    for count in (6, 3, 4, 8, 9, 9, 9, 9, 8, 6, 3, 7):
        sems += [dma((count,)), dma((count,))]
    mixed, col, row = pl.pallas_call(
        functools.partial(kernel, total_tokens, model_width),
        out_shape=(
            jax.ShapeDtypeStruct((block, width), bf16),
            jax.ShapeDtypeStruct((8, 128), f32),
            jax.ShapeDtypeStruct((8, 128), f32),
        ),
        in_specs=[pl.BlockSpec(memory_space=pl.ANY)] * 3,
        out_specs=(pl.BlockSpec(memory_space=pltpu.VMEM),) * 3,
        scratch_shapes=[
            pltpu.VMEM((2, width, units), bf16),
            pltpu.VMEM((units, width), bf16),
            pltpu.VMEM((4, 2, 2, block, width), bf16),
            pltpu.VMEM((4, 2, block, units), f32),
            pltpu.VMEM((4, 2, block, units), bf16),
            pltpu.VMEM((4, 2, block, units), bf16),
            pltpu.VMEM((4, 2, 2, block, half), bf16),
            pltpu.VMEM((4, 2, block, width), f32),
            pltpu.VMEM((4, 2, block, width), bf16),
            pltpu.VMEM((4, block, width), bf16),
            pltpu.VMEM((3, block, width), bf16),
            pltpu.VMEM((3, block, width), bf16),
            pltpu.VMEM((block, width), f32),
            pltpu.VMEM((2, 8, half), f32),
            pltpu.VMEM((4, 2, 8, half), f32),
            pltpu.VMEM((2, 8, half), bf16),
            pltpu.VMEM((4, 2, 16, 128), f32),
            pltpu.VMEM((8, 16, 128), f32),
            dma((8,)),
        ]
        + sems,
        compiler_params=pltpu.CompilerParams(
            collective_id=0, has_side_effects=True, vmem_limit_bytes=56 * 2**20
        ),
        name="swiglu_grid",
    )(tokens, gate_up, down_weight)
    return pl.pallas_call(
        write_results,
        out_shape=(
            jax.ShapeDtypeStruct((block, width), bf16),
            jax.ShapeDtypeStruct((width,), f32),
            jax.ShapeDtypeStruct((block,), f32),
        ),
        name="write_results",
    )(mixed, col, row)


def fits_kernel(mesh):
    return dict(mesh.shape) == {"dp": 2, "row": 4, "col": 4}


def solution(mesh):
    body = per_device_kernel if fits_kernel(mesh) else per_device
    placed = (P(("dp", "col"), "row"), P(None, "row", ("dp", "col")), P(("dp", "col"), "row"))
    return jax.shard_map(
        body,
        mesh=mesh,
        in_specs=placed,
        out_specs=(P(("dp", "col"), "row"), P("row"), P(("dp", "col"))),
        check_vma=False,
    )
```

```python
import functools
import math

import jax
import jax.numpy as jnp
from jax import lax
from jax.experimental import pallas as pl
from jax.experimental.pallas import tpu as pltpu
from jax.sharding import PartitionSpec as P

MESH = pl.DeviceIdType.MESH
TILE = 256


def swiglu(partial_value):
    return (jax.nn.silu(partial_value[:, 0]) * partial_value[:, 1]).astype(jnp.bfloat16)


def hidden_units(partial_value):
    share = lax.psum_scatter(partial_value, "row", scatter_dimension=0, tiled=True)
    return lax.all_gather(swiglu(share), "row", axis=0, tiled=True)


def make_accumulate(hidden, shard_piece):
    columns_wide = hidden.astype(jnp.float32)
    piece_wide = shard_piece.astype(jnp.float32)
    output_part = jnp.dot(hidden, shard_piece, preferred_element_type=jnp.float32)
    column_part = jnp.dot(
        jnp.sum(columns_wide, axis=0), piece_wide, precision=lax.Precision.HIGHEST
    )
    row_part = jnp.dot(columns_wide, jnp.sum(piece_wide, axis=1), precision=lax.Precision.HIGHEST)
    return (output_part, column_part, row_part)


def per_device(tokens, gate_up, down_weight):
    total_tokens = tokens.shape[0] * lax.axis_size(("dp", "col"))
    model_width = tokens.shape[1] * lax.axis_size("row")
    group_rows = lax.all_gather(tokens, "col", axis=0, tiled=True)
    partial_value = jnp.einsum(
        "td,gdf->tgf",
        group_rows,
        lax.all_gather(gate_up, "dp", axis=2, tiled=True),
        preferred_element_type=jnp.float32,
    )
    hidden = hidden_units(partial_value)
    output_part, column_part, row_part = make_accumulate(
        hidden, lax.all_gather(down_weight, "dp", axis=0, tiled=True)
    )
    mixed, row_share = (
        lax.psum_scatter(output_part, "col", scatter_dimension=0, tiled=True),
        lax.psum_scatter(row_part, "col", scatter_dimension=0, tiled=True),
    )
    col_check = lax.psum(column_part, ("dp", "col")) / math.sqrt(total_tokens)
    row_check = lax.psum(row_share, "row") / math.sqrt(model_width)
    return (mixed.astype(jnp.bfloat16), col_check, row_check)


def dot(a, b):
    return jnp.dot(a, b, preferred_element_type=jnp.float32)


def dot_rows(a, b):
    return lax.dot_general(a, b, (((1,), (1,)), ((), ())), preferred_element_type=jnp.float32)


def three_terms(row):
    high = row.astype(jnp.bfloat16)
    rest = row - high.astype(jnp.float32)
    middle = rest.astype(jnp.bfloat16)
    low = (rest - middle.astype(jnp.float32)).astype(jnp.bfloat16)
    index = lax.broadcasted_iota(jnp.int32, row.shape, 0)
    terms = jnp.where(
        index == 0,
        high.astype(jnp.float32),
        jnp.where(
            index == 1,
            middle.astype(jnp.float32),
            jnp.where(index == 2, low.astype(jnp.float32), 0.0),
        ),
    )
    return terms.astype(jnp.bfloat16)


def kernel(
    total_tokens,
    model_width,
    tokens_ref,
    gate_up_ref,
    down_ref,
    mixed_ref,
    col_ref,
    row_ref,
    weights,
    down,
    acts,
    part_wide,
    part_send,
    part_recv,
    hidden,
    out_wide,
    out_send,
    x_recv,
    z_send,
    z_recv,
    own_sum,
    unit_sums,
    weight_parts,
    weight_terms,
    small_send,
    small_recv,
    local_sem,
    w_send,
    w_recv,
    tz_send,
    tz_recv,
    tx_send,
    tx_recv,
    tp_send,
    tp_recv,
    py_send,
    py_recv,
    hp_send,
    hp_recv,
    hy_send,
    hy_recv,
    hf_send,
    hf_recv,
    mx_send,
    mx_recv,
    mz_send,
    mz_recv,
    ws_send,
    ws_recv,
    sm_send,
    sm_recv,
):
    block, width = tokens_ref.shape
    units = down_ref.shape[0]
    half = units // 2
    group = half // 256 * 128
    left = half - 2 * group
    wide, last = 2 * group, 4 * group
    strips = (2, 4, 2, 2)
    x = lax.axis_index("dp")
    row = lax.axis_index("row")
    z = lax.axis_index("col")
    y, core = lax.div(row, 2), lax.rem(row, 2)
    nx, ny, ncore = 1 - x, 1 - y, 1 - core
    zs = [z, z + 1 - 2 * lax.rem(z, 2), lax.rem(z + 2, 4), 3 - z]
    partner = (x, y * 2 + ncore, z)
    across_y = (x, ny * 2 + core, z)
    across_x = (nx, row, z)
    rows = [(x, lax.rem(row + k, 4), z) for k in range(1, 4)]
    peers = [(x, row, zs[j]) for j in range(1, 4)] + [(nx, row, zs[j]) for j in range(4)]
    small_slots = [(j, x) for j in range(1, 4)] + [(j, nx) for j in range(4)]
    sent = []

    def send(src, dst, send_sem, recv_sem, device):
        copy = pltpu.make_async_remote_copy(
            src_ref=src,
            dst_ref=dst,
            send_sem=send_sem,
            recv_sem=recv_sem,
            device_id=device,
            device_id_type=MESH,
        )
        copy.start()
        sent.append(copy)
        return copy

    def weight_slices(which):
        for start, count in ((ny * group, group), (2 * group, left), (y * group, group)):
            for g in range(2):
                lanes = pl.ds(pl.multiple_of(which * half + start, 128), count)
                place = pl.ds(pl.multiple_of(2 * start + g * count, 128), count)
                yield gate_up_ref.at[g, :, lanes], weights.at[core, :, place]

    local = [pltpu.make_async_copy(tokens_ref, acts.at[z, core, x], local_sem.at[0])]
    for k, (src, dst) in enumerate(weight_slices(core)):
        local.append(pltpu.make_async_copy(src, dst, local_sem.at[1 + k]))
    local.append(pltpu.make_async_copy(down_ref, down, local_sem.at[7]))
    for copy in local:
        copy.start()

    barrier = pltpu.get_barrier_semaphore()
    for device in rows + peers:
        pl.semaphore_signal(barrier, inc=1, device_id=device, device_id_type=MESH)
    pl.semaphore_wait(barrier, len(rows) + len(peers))

    tx, tp, tz = {}, {}, {}
    tx[0] = send(tokens_ref, acts.at[z, core, x], tx_send.at[0], tx_recv.at[0], across_x)
    tp[0, 0] = send(tokens_ref, acts.at[z, core, x], tp_send.at[0], tp_recv.at[0], partner)

    def offer(j):
        tz[j] = send(
            tokens_ref, acts.at[z, core, x], tz_send.at[j - 1], tz_recv.at[j - 1], peers[j - 1]
        )

    offer(1)
    swap = [
        send(src, dst, w_send.at[k], w_recv.at[k], partner)
        for k, (src, dst) in enumerate(weight_slices(ncore))
    ]

    unit_sums[...] = jnp.zeros_like(unit_sums)
    weight_parts[row] = jnp.zeros((16, 128), jnp.float32)
    small_send[...] = jnp.zeros_like(small_send)

    weight_copies = []

    def sum_weights():
        local[7].wait()
        ones_width = jnp.ones((8, width), jnp.bfloat16)
        for h in range(2):
            sums = dot_rows(ones_width, down[h * half : (h + 1) * half, :])
            for k in range(half // 128):
                line = slice(8 * h + k, 8 * h + k + 1)
                weight_parts[row, line, :] = sums[0:1, k * 128 : (k + 1) * 128]
        place = weight_parts.at[row]
        for k in range(3):
            weight_copies.append(send(place, place, ws_send.at[k], ws_recv.at[k], rows[k]))

    def total_weights():
        for copy in weight_copies:
            copy.wait_recv()
        total = weight_parts[0] + weight_parts[1] + weight_parts[2] + weight_parts[3]
        for h in range(2):
            sums = jnp.concatenate(
                [total[8 * h + k : 8 * h + k + 1, :] for k in range(half // 128)], axis=1
            )
            weight_terms[h] = three_terms(jnp.broadcast_to(sums, (8, half)))

    def arrive(j):
        tz[j].wait_recv()
        place = acts.at[zs[j], core, x]
        tx[j] = send(place, place, tx_send.at[j], tx_recv.at[j], across_x)
        tp[j, 0] = send(place, place, tp_send.at[2 * j], tp_recv.at[2 * j], partner)

    def arrive_across(j):
        tx[j].wait_recv()
        place = acts.at[zs[j], core, nx]
        tp[j, 1] = send(place, place, tp_send.at[2 * j + 1], tp_recv.at[2 * j + 1], partner)

    py, hp, hy, hf, mx, mz = {}, {}, {}, {}, {}, {}

    def ready(j):
        tp[j, 0].wait_recv()
        tp[j, 1].wait_recv()

    def columns_of(tile):
        return pl.ds(pl.multiple_of(tile * TILE, TILE), TILE)

    def multiply_block(b, tile, tiles):
        def body(t, carry):
            columns = columns_of(tile + t)
            product = dot(acts[z, 0, b], weights[0, :, columns]) + dot(
                acts[z, 1, b], weights[1, :, columns]
            )
            part_send[0, b, :, columns] = product.astype(jnp.bfloat16)
            return carry

        lax.fori_loop(0, tiles, body, 0)

    def multiply(j, tile, tiles):
        def body(t, carry):
            columns = columns_of(tile + t)
            product = dot(
                acts[zs[j], 0].reshape(2 * block, width), weights[0, :, columns]
            ) + dot(acts[zs[j], 1].reshape(2 * block, width), weights[1, :, columns])
            product = product.reshape(2, block, TILE)
            part_wide[j, :, :, columns] = product
            part_send[j, :, :, columns] = product.astype(jnp.bfloat16)
            return carry

        lax.fori_loop(0, tiles, body, 0)

    def send_part(n, j, b, place):
        py[n] = send(
            part_send.at[j, b, :, place],
            part_recv.at[j, b, :, place],
            py_send.at[n],
            py_recv.at[n],
            across_y,
        )

    def at_128(start, count):
        return pl.ds(pl.multiple_of(start, 128), count)

    def terms_of(n):
        if n < 2:
            return 0, [((x, nx)[n], y * wide, group, y * group)]
        if n == 2:
            return 0, [(y, last, left, wide)]
        j, p = divmod(n - 1, 2)
        if p == 0:
            return j, [(y, 0, group, 0)]
        return j, [(y, wide, group, group), (y, last, left, wide)]

    def hidden_place(n, who):
        if n < 2:
            return hidden.at[0, core, (x, nx)[n], :, at_128(who * group, group)]
        if n == 2:
            return hidden.at[0, core, who, :, wide:half]
        j, p = divmod(n - 1, 2)
        lanes = slice(0, group) if p == 0 else slice(group, half)
        return hidden.at[j, core, who, :, lanes]

    def activate(n):
        py[n].wait_recv()
        j, terms = terms_of(n)
        for b, column, count, unit in terms:
            gate, up = [
                part_wide[j, b, :, place] + part_recv[j, b, :, place].astype(jnp.float32)
                for place in (at_128(column, count), at_128(column + count, count))
            ]
            value = gate / (1.0 + jnp.exp(-gate)) * up
            hidden[j, core, b, :, at_128(unit, count)] = value.astype(jnp.bfloat16)
        place = hidden_place(n, y)
        hp[n] = send(place, place, hp_send.at[n], hp_recv.at[n], partner)

    def across(n):
        place = hidden_place(n, y)
        hy[n] = send(place, place, hy_send.at[n], hy_recv.at[n], across_y)

    def hand_over(n):
        hy[n].wait_recv()
        place = hidden_place(n, ny)
        hf[n] = send(place, place, hf_send.at[n], hf_recv.at[n], partner)

    def gate_and_up(j):
        ready(j)
        multiply(j, 0, wide // TILE)
        send_part(1 + 2 * j, j, ny, slice(0, wide))
        multiply(j, wide // TILE, (units - wide) // TILE)
        send_part(2 + 2 * j, j, ny, slice(wide, units))

    def strips_of(j):
        step = width // strips[j]
        return [
            (sum(strips[:j]) + q, slice(q * step, (q + 1) * step)) for q in range(strips[j])
        ]

    def send_across(j, n, place):
        mx[n] = send(
            out_send.at[j, nx, :, place],
            x_recv.at[j, :, place],
            mx_send.at[n],
            mx_recv.at[n],
            across_x,
        )

    def down_part(j):
        for n in (1 + 2 * j, 2 + 2 * j):
            hp[n].wait_recv()
            hf[n].wait_recv()

        def body(t, carry):
            columns = columns_of(t)
            product = dot(
                hidden[j, 0].reshape(2 * block, half), down[0:half, columns]
            ) + dot(hidden[j, 1].reshape(2 * block, half), down[half:units, columns])
            product = product.reshape(2, block, TILE)
            out_wide[j, :, :, columns] = product
            out_send[j, :, :, columns] = product.astype(jnp.bfloat16)
            return carry

        for n, place in strips_of(j):
            lax.fori_loop(place.start // TILE, place.stop // TILE, body, 0)
            send_across(j, n, place)

    def down_block(b, place):
        def body(t, carry):
            columns = columns_of(t)
            product = dot(hidden[0, 0, b], down[0:half, columns]) + dot(
                hidden[0, 1, b], down[half:units, columns]
            )
            out_wide[0, b, :, columns] = product
            out_send[0, b, :, columns] = product.astype(jnp.bfloat16)
            return carry

        lax.fori_loop(place.start // TILE, place.stop // TILE, body, 0)

    def down_across():
        for n in (1, 2):
            hp[n].wait_recv()
            hf[n].wait_recv()
        for n, place in strips_of(0):
            down_block(nx, place)
            send_across(0, n, place)

    def down_own():
        hp[0].wait_recv()
        hf[0].wait_recv()
        down_block(x, slice(0, width))

    def checks(j):
        ones = jnp.ones((8, 2 * block), jnp.bfloat16)
        for h in range(2):
            unit_sums[h] += dot(ones, hidden[j, h].reshape(2 * block, half))
        for b in range(2):
            terms = dot_rows(weight_terms[0], hidden[j, 0, b]) + dot_rows(
                weight_terms[1], hidden[j, 1, b]
            )
            small_send[j, b, 8:9, 0:block] = jnp.sum(terms, axis=0, keepdims=True)

    def add_across(j):
        for n, place in strips_of(j):
            mx[n].wait_recv()
            value = out_wide[j, x, :, place] + x_recv[j, :, place].astype(jnp.float32)
            if j == 0:
                own_sum[:, place] = value
            else:
                z_send[j - 1, :, place] = value.astype(jnp.bfloat16)
                mz[n] = send(
                    z_send.at[j - 1, :, place],
                    z_recv.at[j - 1, :, place],
                    mz_send.at[n - strips[0]],
                    mz_recv.at[n - strips[0]],
                    peers[j - 1],
                )

    def weights_here(p):
        for k in (2 * p, 2 * p + 1):
            local[1 + k].wait()
            swap[k].wait_recv()

    local[0].wait()
    tp[0, 0].wait_recv()
    weights_here(0)
    multiply_block(x, ny * (wide // TILE), wide // TILE)
    send_part(0, 0, x, at_128(ny * wide, wide))
    offer(2)
    arrive_across(0)
    arrive(1)
    tp[0, 1].wait_recv()
    multiply_block(nx, ny * (wide // TILE), wide // TILE)
    send_part(1, 0, nx, at_128(ny * wide, wide))
    weights_here(1)
    multiply(0, last // TILE, 2 * left // TILE)
    send_part(2, 0, ny, slice(last, units))
    weights_here(2)
    multiply(0, y * (wide // TILE), wide // TILE)
    sum_weights()
    activate(0)
    activate(1)
    across(1)
    arrive_across(1)
    gate_and_up(1)
    activate(2)
    arrive(2)
    offer(3)
    total_weights()
    hand_over(1)
    activate(3)
    arrive_across(2)
    gate_and_up(2)
    activate(4)
    arrive(3)
    activate(5)
    across(5)
    arrive_across(3)
    gate_and_up(3)
    activate(6)
    across(6)
    across(3)
    hand_over(5)
    hand_over(6)
    down_part(2)
    activate(7)
    across(7)
    activate(8)
    across(8)
    across(4)
    across(2)
    across(0)
    add_across(2)
    checks(2)
    hand_over(3)
    hand_over(7)
    hand_over(8)
    down_part(3)
    hand_over(4)
    down_part(1)
    add_across(3)
    hand_over(2)
    down_across()
    checks(3)
    add_across(1)
    checks(1)
    hand_over(0)
    down_own()
    checks(0)

    column_terms = dot(three_terms(unit_sums[0]), down[0:half, :]) + dot(
        three_terms(unit_sums[1]), down[half:units, :]
    )
    columns = jnp.sum(column_terms, axis=0, keepdims=True)
    for j in range(4):
        for b in range(2):
            for k in range(width // 128):
                small_send[j, b, k : k + 1, :] = columns[:, k * 128 : (k + 1) * 128]
    me = x * 4 + z
    small_recv[me] = small_send[0, x]
    small = [
        send(
            small_send.at[slot[0], slot[1]],
            small_recv.at[me],
            sm_send.at[k],
            sm_recv.at[k],
            peers[k],
        )
        for k, slot in enumerate(small_slots)
    ]
    add_across(0)
    for copy in small:
        copy.wait_recv()
    total = small_recv[0]
    for k in range(1, 8):
        total = total + small_recv[k]
    col_ref[...] = total[0:8] / math.sqrt(total_tokens)
    row_ref[...] = total[8:16] / math.sqrt(model_width)
    for j in range(1, 4):
        for n, _ in strips_of(j):
            mz[n].wait_recv()
    mixed_ref[...] = (
        own_sum[...]
        + z_recv[0].astype(jnp.float32)
        + z_recv[1].astype(jnp.float32)
        + z_recv[2].astype(jnp.float32)
    ).astype(jnp.bfloat16)
    for copy in sent:
        copy.wait_send()


def write_results(mixed_ref, col_ref, row_ref, mixed_out, col_out, row_out):
    mixed_out[...] = mixed_ref[...]
    for k in range(col_ref.shape[0]):
        col_out[pl.ds(k * 128, 128)] = col_ref[k]
    row_out[...] = row_ref[0, 0 : row_out.shape[0]]


def per_device_kernel(tokens, gate_up, down_weight):
    block, width = tokens.shape
    units = down_weight.shape[0]
    half = units // 2
    total_tokens = block * lax.axis_size(("dp", "col"))
    model_width = width * lax.axis_size("row")
    dma = pltpu.SemaphoreType.DMA
    bf16, f32 = jnp.bfloat16, jnp.float32
    sems = []
    for count in (6, 3, 4, 8, 9, 9, 9, 9, 10, 8, 3, 7):
        sems += [dma((count,)), dma((count,))]
    mixed, col, row = pl.pallas_call(
        functools.partial(kernel, total_tokens, model_width),
        out_shape=(
            jax.ShapeDtypeStruct((block, width), bf16),
            jax.ShapeDtypeStruct((8, 128), f32),
            jax.ShapeDtypeStruct((8, 128), f32),
        ),
        in_specs=[pl.BlockSpec(memory_space=pl.ANY)] * 3,
        out_specs=(pl.BlockSpec(memory_space=pltpu.VMEM),) * 3,
        scratch_shapes=[
            pltpu.VMEM((2, width, units), bf16),
            pltpu.VMEM((units, width), bf16),
            pltpu.VMEM((4, 2, 2, block, width), bf16),
            pltpu.VMEM((4, 2, block, units), f32),
            pltpu.VMEM((4, 2, block, units), bf16),
            pltpu.VMEM((4, 2, block, units), bf16),
            pltpu.VMEM((4, 2, 2, block, half), bf16),
            pltpu.VMEM((4, 2, block, width), f32),
            pltpu.VMEM((4, 2, block, width), bf16),
            pltpu.VMEM((4, block, width), bf16),
            pltpu.VMEM((3, block, width), bf16),
            pltpu.VMEM((3, block, width), bf16),
            pltpu.VMEM((block, width), f32),
            pltpu.VMEM((2, 8, half), f32),
            pltpu.VMEM((4, 16, 128), f32),
            pltpu.VMEM((2, 8, half), bf16),
            pltpu.VMEM((4, 2, 16, 128), f32),
            pltpu.VMEM((8, 16, 128), f32),
            dma((8,)),
        ]
        + sems,
        compiler_params=pltpu.CompilerParams(
            collective_id=0, has_side_effects=True, vmem_limit_bytes=56 * 2**20
        ),
        name="swiglu_grid",
    )(tokens, gate_up, down_weight)
    return pl.pallas_call(
        write_results,
        out_shape=(
            jax.ShapeDtypeStruct((block, width), bf16),
            jax.ShapeDtypeStruct((width,), f32),
            jax.ShapeDtypeStruct((block,), f32),
        ),
        name="write_results",
    )(mixed, col, row)


def fits_kernel(mesh):
    return dict(mesh.shape) == {"dp": 2, "row": 4, "col": 4}


def solution(mesh):
    body = per_device_kernel if fits_kernel(mesh) else per_device
    placed = (P(("dp", "col"), "row"), P(None, "row", ("dp", "col")), P(("dp", "col"), "row"))
    return jax.shard_map(
        body,
        mesh=mesh,
        in_specs=placed,
        out_specs=(P(("dp", "col"), "row"), P("row"), P(("dp", "col"))),
        check_vma=False,
    )
```

```python
import functools
import math

import jax
import jax.numpy as jnp
from jax import lax
from jax.experimental import pallas as pl
from jax.experimental.pallas import tpu as pltpu
from jax.sharding import PartitionSpec as P

MESH = pl.DeviceIdType.MESH
TILE = 256


def swiglu(partial_value):
    return (jax.nn.silu(partial_value[:, 0]) * partial_value[:, 1]).astype(jnp.bfloat16)


def hidden_units(partial_value):
    share = lax.psum_scatter(partial_value, "row", scatter_dimension=0, tiled=True)
    return lax.all_gather(swiglu(share), "row", axis=0, tiled=True)


def make_accumulate(hidden, shard_piece):
    columns_wide = hidden.astype(jnp.float32)
    piece_wide = shard_piece.astype(jnp.float32)
    output_part = jnp.dot(hidden, shard_piece, preferred_element_type=jnp.float32)
    column_part = jnp.dot(
        jnp.sum(columns_wide, axis=0), piece_wide, precision=lax.Precision.HIGHEST
    )
    row_part = jnp.dot(columns_wide, jnp.sum(piece_wide, axis=1), precision=lax.Precision.HIGHEST)
    return (output_part, column_part, row_part)


def per_device(tokens, gate_up, down_weight):
    total_tokens = tokens.shape[0] * lax.axis_size(("dp", "col"))
    model_width = tokens.shape[1] * lax.axis_size("row")
    group_rows = lax.all_gather(tokens, "col", axis=0, tiled=True)
    partial_value = jnp.einsum(
        "td,gdf->tgf",
        group_rows,
        lax.all_gather(gate_up, "dp", axis=2, tiled=True),
        preferred_element_type=jnp.float32,
    )
    hidden = hidden_units(partial_value)
    output_part, column_part, row_part = make_accumulate(
        hidden, lax.all_gather(down_weight, "dp", axis=0, tiled=True)
    )
    mixed, row_share = (
        lax.psum_scatter(output_part, "col", scatter_dimension=0, tiled=True),
        lax.psum_scatter(row_part, "col", scatter_dimension=0, tiled=True),
    )
    col_check = lax.psum(column_part, ("dp", "col")) / math.sqrt(total_tokens)
    row_check = lax.psum(row_share, "row") / math.sqrt(model_width)
    return (mixed.astype(jnp.bfloat16), col_check, row_check)


def dot(a, b):
    return jnp.dot(a, b, preferred_element_type=jnp.float32)


def dot_rows(a, b):
    return lax.dot_general(a, b, (((1,), (1,)), ((), ())), preferred_element_type=jnp.float32)


def three_terms(row):
    high = row.astype(jnp.bfloat16)
    rest = row - high.astype(jnp.float32)
    middle = rest.astype(jnp.bfloat16)
    low = (rest - middle.astype(jnp.float32)).astype(jnp.bfloat16)
    index = lax.broadcasted_iota(jnp.int32, row.shape, 0)
    terms = jnp.where(
        index == 0,
        high.astype(jnp.float32),
        jnp.where(
            index == 1,
            middle.astype(jnp.float32),
            jnp.where(index == 2, low.astype(jnp.float32), 0.0),
        ),
    )
    return terms.astype(jnp.bfloat16)


def kernel(
    total_tokens,
    model_width,
    tokens_ref,
    gate_up_ref,
    down_ref,
    mixed_ref,
    col_ref,
    row_ref,
    weights,
    down,
    acts,
    part_wide,
    part_send,
    part_recv,
    hidden,
    out_wide,
    out_send,
    x_recv,
    z_send,
    z_recv,
    own_sum,
    unit_sums,
    weight_parts,
    weight_terms,
    small_send,
    small_recv,
    local_sem,
    w_send,
    w_recv,
    tz_send,
    tz_recv,
    tx_send,
    tx_recv,
    tp_send,
    tp_recv,
    py_send,
    py_recv,
    hp_send,
    hp_recv,
    hy_send,
    hy_recv,
    hf_send,
    hf_recv,
    mx_send,
    mx_recv,
    mz_send,
    mz_recv,
    ws_send,
    ws_recv,
    sm_send,
    sm_recv,
):
    block, width = tokens_ref.shape
    units = down_ref.shape[0]
    half = units // 2
    group = half // 256 * 128
    left = half - 2 * group
    wide, last = 2 * group, 4 * group
    strips = (2, 4, 2, 2)
    x = lax.axis_index("dp")
    row = lax.axis_index("row")
    z = lax.axis_index("col")
    y, core = lax.div(row, 2), lax.rem(row, 2)
    nx, ny, ncore = 1 - x, 1 - y, 1 - core
    zs = [z, z + 1 - 2 * lax.rem(z, 2), lax.rem(z + 2, 4), 3 - z]
    partner = (x, y * 2 + ncore, z)
    across_y = (x, ny * 2 + core, z)
    across_x = (nx, row, z)
    rows = [(x, lax.rem(row + k, 4), z) for k in range(1, 4)]
    peers = [(x, row, zs[j]) for j in range(1, 4)] + [(nx, row, zs[j]) for j in range(4)]
    small_slots = [(j, x) for j in range(1, 4)] + [(j, nx) for j in range(4)]
    sent = []

    def send(src, dst, send_sem, recv_sem, device):
        copy = pltpu.make_async_remote_copy(
            src_ref=src,
            dst_ref=dst,
            send_sem=send_sem,
            recv_sem=recv_sem,
            device_id=device,
            device_id_type=MESH,
        )
        copy.start()
        sent.append(copy)
        return copy

    def weight_slices(which):
        for start, count in ((ny * group, group), (2 * group, left), (y * group, group)):
            for g in range(2):
                lanes = pl.ds(pl.multiple_of(which * half + start, 128), count)
                place = pl.ds(pl.multiple_of(2 * start + g * count, 128), count)
                yield gate_up_ref.at[g, :, lanes], weights.at[core, :, place]

    local = [pltpu.make_async_copy(tokens_ref, acts.at[z, core, x], local_sem.at[0])]
    for k, (src, dst) in enumerate(weight_slices(core)):
        local.append(pltpu.make_async_copy(src, dst, local_sem.at[1 + k]))
    local.append(pltpu.make_async_copy(down_ref, down, local_sem.at[7]))
    for copy in local:
        copy.start()

    barrier = pltpu.get_barrier_semaphore()
    for device in rows + peers:
        pl.semaphore_signal(barrier, inc=1, device_id=device, device_id_type=MESH)
    pl.semaphore_wait(barrier, len(rows) + len(peers))

    tx, tp, tz = {}, {}, {}
    tx[0] = send(tokens_ref, acts.at[z, core, x], tx_send.at[0], tx_recv.at[0], across_x)
    tp[0, 0] = send(tokens_ref, acts.at[z, core, x], tp_send.at[0], tp_recv.at[0], partner)

    def offer(j):
        tz[j] = send(
            tokens_ref, acts.at[z, core, x], tz_send.at[j - 1], tz_recv.at[j - 1], peers[j - 1]
        )

    offer(2)
    swap = [
        send(src, dst, w_send.at[k], w_recv.at[k], partner)
        for k, (src, dst) in enumerate(weight_slices(ncore))
    ]

    unit_sums[...] = jnp.zeros_like(unit_sums)
    weight_parts[row] = jnp.zeros((16, 128), jnp.float32)
    small_send[...] = jnp.zeros_like(small_send)

    weight_copies = []

    def sum_weights():
        local[7].wait()
        ones_width = jnp.ones((8, width), jnp.bfloat16)
        for h in range(2):
            sums = dot_rows(ones_width, down[h * half : (h + 1) * half, :])
            for k in range(half // 128):
                line = slice(8 * h + k, 8 * h + k + 1)
                weight_parts[row, line, :] = sums[0:1, k * 128 : (k + 1) * 128]
        place = weight_parts.at[row]
        for k in range(3):
            weight_copies.append(send(place, place, ws_send.at[k], ws_recv.at[k], rows[k]))

    def total_weights():
        for copy in weight_copies:
            copy.wait_recv()
        total = weight_parts[0] + weight_parts[1] + weight_parts[2] + weight_parts[3]
        for h in range(2):
            sums = jnp.concatenate(
                [total[8 * h + k : 8 * h + k + 1, :] for k in range(half // 128)], axis=1
            )
            weight_terms[h] = three_terms(jnp.broadcast_to(sums, (8, half)))

    def arrive(j):
        tz[j].wait_recv()
        place = acts.at[zs[j], core, x]
        tx[j] = send(place, place, tx_send.at[j], tx_recv.at[j], across_x)
        tp[j, 0] = send(place, place, tp_send.at[2 * j], tp_recv.at[2 * j], partner)

    def arrive_across(j):
        tx[j].wait_recv()
        place = acts.at[zs[j], core, nx]
        tp[j, 1] = send(place, place, tp_send.at[2 * j + 1], tp_recv.at[2 * j + 1], partner)

    py, hp, hy, hf, mx, mz = {}, {}, {}, {}, {}, {}

    def ready(j):
        tp[j, 0].wait_recv()
        tp[j, 1].wait_recv()

    def columns_of(tile):
        return pl.ds(pl.multiple_of(tile * TILE, TILE), TILE)

    def multiply_block(b, tile, tiles):
        def body(t, carry):
            columns = columns_of(tile + t)
            product = dot(acts[z, 0, b], weights[0, :, columns]) + dot(
                acts[z, 1, b], weights[1, :, columns]
            )
            part_send[0, b, :, columns] = product.astype(jnp.bfloat16)
            return carry

        lax.fori_loop(0, tiles, body, 0)

    def multiply(j, tile, tiles):
        def body(t, carry):
            columns = columns_of(tile + t)
            product = dot(
                acts[zs[j], 0].reshape(2 * block, width), weights[0, :, columns]
            ) + dot(acts[zs[j], 1].reshape(2 * block, width), weights[1, :, columns])
            product = product.reshape(2, block, TILE)
            part_wide[j, :, :, columns] = product
            part_send[j, :, :, columns] = product.astype(jnp.bfloat16)
            return carry

        lax.fori_loop(0, tiles, body, 0)

    def send_part(n, j, b, place):
        py[n] = send(
            part_send.at[j, b, :, place],
            part_recv.at[j, b, :, place],
            py_send.at[n],
            py_recv.at[n],
            across_y,
        )

    def at_128(start, count):
        return pl.ds(pl.multiple_of(start, 128), count)

    def terms_of(n):
        if n < 2:
            return 0, [((x, nx)[n], y * wide, group, y * group)]
        if n == 2:
            return 0, [(y, last, left, wide)]
        j, p = divmod(n - 1, 2)
        if p == 0:
            return j, [(y, 0, group, 0)]
        return j, [(y, wide, group, group), (y, last, left, wide)]

    def hidden_place(n, who):
        if n < 2:
            return hidden.at[0, core, (x, nx)[n], :, at_128(who * group, group)]
        if n == 2:
            return hidden.at[0, core, who, :, wide:half]
        j, p = divmod(n - 1, 2)
        lanes = slice(0, group) if p == 0 else slice(group, half)
        return hidden.at[j, core, who, :, lanes]

    def activate(n):
        py[n].wait_recv()
        j, terms = terms_of(n)
        for b, column, count, unit in terms:
            gate, up = [
                part_wide[j, b, :, place] + part_recv[j, b, :, place].astype(jnp.float32)
                for place in (at_128(column, count), at_128(column + count, count))
            ]
            value = gate / (1.0 + jnp.exp(-gate)) * up
            hidden[j, core, b, :, at_128(unit, count)] = value.astype(jnp.bfloat16)
        place = hidden_place(n, y)
        hp[n] = send(place, place, hp_send.at[n], hp_recv.at[n], partner)

    def across(n):
        place = hidden_place(n, y)
        hy[n] = send(place, place, hy_send.at[n], hy_recv.at[n], across_y)

    def hand_over(n):
        hy[n].wait_recv()
        place = hidden_place(n, ny)
        hf[n] = send(place, place, hf_send.at[n], hf_recv.at[n], partner)

    def gate_and_up(j):
        ready(j)
        multiply(j, 0, wide // TILE)
        send_part(1 + 2 * j, j, ny, slice(0, wide))
        multiply(j, wide // TILE, (units - wide) // TILE)

    def send_rest(j):
        send_part(2 + 2 * j, j, ny, slice(wide, units))

    def strips_of(j):
        step = width // strips[j]
        return [
            (sum(strips[:j]) + q, slice(q * step, (q + 1) * step)) for q in range(strips[j])
        ]

    def send_across(j, n, place):
        mx[n] = send(
            out_send.at[j, nx, :, place],
            x_recv.at[j, :, place],
            mx_send.at[n],
            mx_recv.at[n],
            across_x,
        )

    def down_part(j):
        for n in (1 + 2 * j, 2 + 2 * j):
            hp[n].wait_recv()
            hf[n].wait_recv()

        def body(t, carry):
            columns = columns_of(t)
            product = dot(
                hidden[j, 0].reshape(2 * block, half), down[0:half, columns]
            ) + dot(hidden[j, 1].reshape(2 * block, half), down[half:units, columns])
            product = product.reshape(2, block, TILE)
            out_wide[j, :, :, columns] = product
            out_send[j, :, :, columns] = product.astype(jnp.bfloat16)
            return carry

        for n, place in strips_of(j):
            lax.fori_loop(place.start // TILE, place.stop // TILE, body, 0)
            send_across(j, n, place)

    def down_block(b, place):
        def body(t, carry):
            columns = columns_of(t)
            product = dot(hidden[0, 0, b], down[0:half, columns]) + dot(
                hidden[0, 1, b], down[half:units, columns]
            )
            out_wide[0, b, :, columns] = product
            out_send[0, b, :, columns] = product.astype(jnp.bfloat16)
            return carry

        lax.fori_loop(place.start // TILE, place.stop // TILE, body, 0)

    def down_across():
        for n in (1, 2):
            hp[n].wait_recv()
            hf[n].wait_recv()
        for n, place in strips_of(0):
            down_block(nx, place)
            send_across(0, n, place)

    def down_own():
        hp[0].wait_recv()
        hf[0].wait_recv()
        down_block(x, slice(0, width))

    def checks(j):
        ones = jnp.ones((8, 2 * block), jnp.bfloat16)
        for h in range(2):
            unit_sums[h] += dot(ones, hidden[j, h].reshape(2 * block, half))
        for b in range(2):
            terms = dot_rows(weight_terms[0], hidden[j, 0, b]) + dot_rows(
                weight_terms[1], hidden[j, 1, b]
            )
            small_send[j, b, 8:9, 0:block] = jnp.sum(terms, axis=0, keepdims=True)

    def add_across(j):
        for n, place in strips_of(j):
            mx[n].wait_recv()
            value = out_wide[j, x, :, place] + x_recv[j, :, place].astype(jnp.float32)
            if j == 0:
                own_sum[:, place] = value
            else:
                z_send[j - 1, :, place] = value.astype(jnp.bfloat16)
                mz[n] = send(
                    z_send.at[j - 1, :, place],
                    z_recv.at[j - 1, :, place],
                    mz_send.at[n - strips[0]],
                    mz_recv.at[n - strips[0]],
                    peers[j - 1],
                )

    def weights_here(p):
        for k in (2 * p, 2 * p + 1):
            local[1 + k].wait()
            swap[k].wait_recv()

    local[0].wait()
    tp[0, 0].wait_recv()
    weights_here(0)
    multiply_block(x, ny * (wide // TILE), wide // TILE)
    send_part(0, 0, x, at_128(ny * wide, wide))
    arrive_across(0)
    tp[0, 1].wait_recv()
    multiply_block(nx, ny * (wide // TILE), wide // TILE)
    send_part(1, 0, nx, at_128(ny * wide, wide))
    weights_here(1)
    multiply(0, last // TILE, 2 * left // TILE)
    send_part(2, 0, ny, slice(last, units))
    offer(3)
    weights_here(2)
    multiply(0, y * (wide // TILE), wide // TILE)
    sum_weights()
    activate(0)
    across(0)
    arrive(2)
    offer(1)
    activate(1)
    across(1)
    activate(2)
    across(2)
    arrive_across(2)
    gate_and_up(2)
    send_rest(2)
    total_weights()
    hand_over(0)
    hand_over(1)
    hand_over(2)
    arrive(3)
    activate(5)
    across(5)
    arrive_across(3)
    gate_and_up(3)
    send_rest(3)
    arrive(1)
    activate(6)
    across(6)
    down_across()
    down_own()
    arrive_across(1)
    gate_and_up(1)
    activate(7)
    across(7)
    activate(8)
    across(8)
    send_rest(1)
    hand_over(5)
    hand_over(6)
    down_part(2)
    activate(3)
    across(3)
    checks(0)
    add_across(0)
    hand_over(7)
    hand_over(8)
    down_part(3)
    add_across(2)
    activate(4)
    across(4)
    checks(2)
    checks(3)
    add_across(3)
    hand_over(3)
    hand_over(4)
    down_part(1)
    checks(1)

    column_terms = dot(three_terms(unit_sums[0]), down[0:half, :]) + dot(
        three_terms(unit_sums[1]), down[half:units, :]
    )
    columns = jnp.sum(column_terms, axis=0, keepdims=True)
    for j in range(4):
        for b in range(2):
            for k in range(width // 128):
                small_send[j, b, k : k + 1, :] = columns[:, k * 128 : (k + 1) * 128]
    me = x * 4 + z
    small_recv[me] = small_send[0, x]
    small = [
        send(
            small_send.at[slot[0], slot[1]],
            small_recv.at[me],
            sm_send.at[k],
            sm_recv.at[k],
            peers[k],
        )
        for k, slot in enumerate(small_slots)
    ]
    add_across(1)
    for copy in small:
        copy.wait_recv()
    total = small_recv[0]
    for k in range(1, 8):
        total = total + small_recv[k]
    col_ref[...] = total[0:8] / math.sqrt(total_tokens)
    row_ref[...] = total[8:16] / math.sqrt(model_width)
    for j in range(1, 4):
        for n, _ in strips_of(j):
            mz[n].wait_recv()
    mixed_ref[...] = (
        own_sum[...]
        + z_recv[0].astype(jnp.float32)
        + z_recv[1].astype(jnp.float32)
        + z_recv[2].astype(jnp.float32)
    ).astype(jnp.bfloat16)
    for copy in sent:
        copy.wait_send()


def write_results(mixed_ref, col_ref, row_ref, mixed_out, col_out, row_out):
    mixed_out[...] = mixed_ref[...]
    for k in range(col_ref.shape[0]):
        col_out[pl.ds(k * 128, 128)] = col_ref[k]
    row_out[...] = row_ref[0, 0 : row_out.shape[0]]


def per_device_kernel(tokens, gate_up, down_weight):
    block, width = tokens.shape
    units = down_weight.shape[0]
    half = units // 2
    total_tokens = block * lax.axis_size(("dp", "col"))
    model_width = width * lax.axis_size("row")
    dma = pltpu.SemaphoreType.DMA
    bf16, f32 = jnp.bfloat16, jnp.float32
    sems = []
    for count in (6, 3, 4, 8, 9, 9, 9, 9, 10, 8, 3, 7):
        sems += [dma((count,)), dma((count,))]
    mixed, col, row = pl.pallas_call(
        functools.partial(kernel, total_tokens, model_width),
        out_shape=(
            jax.ShapeDtypeStruct((block, width), bf16),
            jax.ShapeDtypeStruct((8, 128), f32),
            jax.ShapeDtypeStruct((8, 128), f32),
        ),
        in_specs=[pl.BlockSpec(memory_space=pl.ANY)] * 3,
        out_specs=(pl.BlockSpec(memory_space=pltpu.VMEM),) * 3,
        scratch_shapes=[
            pltpu.VMEM((2, width, units), bf16),
            pltpu.VMEM((units, width), bf16),
            pltpu.VMEM((4, 2, 2, block, width), bf16),
            pltpu.VMEM((4, 2, block, units), f32),
            pltpu.VMEM((4, 2, block, units), bf16),
            pltpu.VMEM((4, 2, block, units), bf16),
            pltpu.VMEM((4, 2, 2, block, half), bf16),
            pltpu.VMEM((4, 2, block, width), f32),
            pltpu.VMEM((4, 2, block, width), bf16),
            pltpu.VMEM((4, block, width), bf16),
            pltpu.VMEM((3, block, width), bf16),
            pltpu.VMEM((3, block, width), bf16),
            pltpu.VMEM((block, width), f32),
            pltpu.VMEM((2, 8, half), f32),
            pltpu.VMEM((4, 16, 128), f32),
            pltpu.VMEM((2, 8, half), bf16),
            pltpu.VMEM((4, 2, 16, 128), f32),
            pltpu.VMEM((8, 16, 128), f32),
            dma((8,)),
        ]
        + sems,
        compiler_params=pltpu.CompilerParams(
            collective_id=0, has_side_effects=True, vmem_limit_bytes=56 * 2**20
        ),
        name="swiglu_grid",
    )(tokens, gate_up, down_weight)
    return pl.pallas_call(
        write_results,
        out_shape=(
            jax.ShapeDtypeStruct((block, width), bf16),
            jax.ShapeDtypeStruct((width,), f32),
            jax.ShapeDtypeStruct((block,), f32),
        ),
        name="write_results",
    )(mixed, col, row)


def fits_kernel(mesh):
    return dict(mesh.shape) == {"dp": 2, "row": 4, "col": 4}


def solution(mesh):
    body = per_device_kernel if fits_kernel(mesh) else per_device
    placed = (P(("dp", "col"), "row"), P(None, "row", ("dp", "col")), P(("dp", "col"), "row"))
    return jax.shard_map(
        body,
        mesh=mesh,
        in_specs=placed,
        out_specs=(P(("dp", "col"), "row"), P("row"), P(("dp", "col"))),
        check_vma=False,
    )
```

```python
import functools
import math

import jax
import jax.numpy as jnp
from jax import lax
from jax.experimental import pallas as pl
from jax.experimental.pallas import tpu as pltpu
from jax.sharding import PartitionSpec as P

MESH = pl.DeviceIdType.MESH
TILE = 256


def swiglu(partial_value):
    return (jax.nn.silu(partial_value[:, 0]) * partial_value[:, 1]).astype(jnp.bfloat16)


def hidden_units(partial_value):
    share = lax.psum_scatter(partial_value, "row", scatter_dimension=0, tiled=True)
    return lax.all_gather(swiglu(share), "row", axis=0, tiled=True)


def make_accumulate(hidden, shard_piece):
    columns_wide = hidden.astype(jnp.float32)
    piece_wide = shard_piece.astype(jnp.float32)
    output_part = jnp.dot(hidden, shard_piece, preferred_element_type=jnp.float32)
    column_part = jnp.dot(
        jnp.sum(columns_wide, axis=0), piece_wide, precision=lax.Precision.HIGHEST
    )
    row_part = jnp.dot(columns_wide, jnp.sum(piece_wide, axis=1), precision=lax.Precision.HIGHEST)
    return (output_part, column_part, row_part)


def per_device(tokens, gate_up, down_weight):
    total_tokens = tokens.shape[0] * lax.axis_size(("dp", "col"))
    model_width = tokens.shape[1] * lax.axis_size("row")
    group_rows = lax.all_gather(tokens, "col", axis=0, tiled=True)
    partial_value = jnp.einsum(
        "td,gdf->tgf",
        group_rows,
        lax.all_gather(gate_up, "dp", axis=2, tiled=True),
        preferred_element_type=jnp.float32,
    )
    hidden = hidden_units(partial_value)
    output_part, column_part, row_part = make_accumulate(
        hidden, lax.all_gather(down_weight, "dp", axis=0, tiled=True)
    )
    mixed, row_share = (
        lax.psum_scatter(output_part, "col", scatter_dimension=0, tiled=True),
        lax.psum_scatter(row_part, "col", scatter_dimension=0, tiled=True),
    )
    col_check = lax.psum(column_part, ("dp", "col")) / math.sqrt(total_tokens)
    row_check = lax.psum(row_share, "row") / math.sqrt(model_width)
    return (mixed.astype(jnp.bfloat16), col_check, row_check)


def dot(a, b):
    return jnp.dot(a, b, preferred_element_type=jnp.float32)


def dot_rows(a, b):
    return lax.dot_general(a, b, (((1,), (1,)), ((), ())), preferred_element_type=jnp.float32)


def three_terms(row):
    high = row.astype(jnp.bfloat16)
    rest = row - high.astype(jnp.float32)
    middle = rest.astype(jnp.bfloat16)
    low = (rest - middle.astype(jnp.float32)).astype(jnp.bfloat16)
    index = lax.broadcasted_iota(jnp.int32, row.shape, 0)
    terms = jnp.where(
        index == 0,
        high.astype(jnp.float32),
        jnp.where(
            index == 1,
            middle.astype(jnp.float32),
            jnp.where(index == 2, low.astype(jnp.float32), 0.0),
        ),
    )
    return terms.astype(jnp.bfloat16)


def kernel(
    total_tokens,
    model_width,
    tokens_ref,
    gate_up_ref,
    down_ref,
    mixed_ref,
    col_ref,
    row_ref,
    weights,
    down,
    acts,
    part_wide,
    part_send,
    part_recv,
    hidden,
    out_wide,
    out_send,
    x_recv,
    z_send,
    z_recv,
    own_sum,
    unit_sums,
    weight_parts,
    weight_terms,
    small_send,
    small_recv,
    unit_terms,
    column_sums,
    local_sem,
    w_send,
    w_recv,
    tz_send,
    tz_recv,
    tx_send,
    tx_recv,
    tp_send,
    tp_recv,
    py_send,
    py_recv,
    hp_send,
    hp_recv,
    hy_send,
    hy_recv,
    hf_send,
    hf_recv,
    mx_send,
    mx_recv,
    mz_send,
    mz_recv,
    ws_send,
    ws_recv,
    sm_send,
    sm_recv,
):
    block, width = tokens_ref.shape
    units = down_ref.shape[0]
    half = units // 2
    group = half // 256 * 128
    left = half - 2 * group
    wide, last = 2 * group, 4 * group
    strips = (2, 4, 2, 2)
    x = lax.axis_index("dp")
    row = lax.axis_index("row")
    z = lax.axis_index("col")
    y, core = lax.div(row, 2), lax.rem(row, 2)
    nx, ny, ncore = 1 - x, 1 - y, 1 - core
    zs = [z, z + 1 - 2 * lax.rem(z, 2), lax.rem(z + 2, 4), 3 - z]
    partner = (x, y * 2 + ncore, z)
    across_y = (x, ny * 2 + core, z)
    across_x = (nx, row, z)
    rows = [(x, lax.rem(row + k, 4), z) for k in range(1, 4)]
    peers = [(x, row, zs[j]) for j in range(1, 4)] + [(nx, row, zs[j]) for j in range(4)]
    small_slots = [(j, x) for j in range(1, 4)] + [(j, nx) for j in range(4)]
    sent = []

    def send(src, dst, send_sem, recv_sem, device):
        copy = pltpu.make_async_remote_copy(
            src_ref=src,
            dst_ref=dst,
            send_sem=send_sem,
            recv_sem=recv_sem,
            device_id=device,
            device_id_type=MESH,
        )
        copy.start()
        sent.append(copy)
        return copy

    def weight_slices(which):
        for start, count in ((ny * group, group), (2 * group, left), (y * group, group)):
            for g in range(2):
                lanes = pl.ds(pl.multiple_of(which * half + start, 128), count)
                place = pl.ds(pl.multiple_of(2 * start + g * count, 128), count)
                yield gate_up_ref.at[g, :, lanes], weights.at[core, :, place]

    local = [pltpu.make_async_copy(tokens_ref, acts.at[z, core, x], local_sem.at[0])]
    for k, (src, dst) in enumerate(weight_slices(core)):
        local.append(pltpu.make_async_copy(src, dst, local_sem.at[1 + k]))
    local.append(pltpu.make_async_copy(down_ref, down, local_sem.at[7]))
    for copy in local:
        copy.start()

    barrier = pltpu.get_barrier_semaphore()
    for device in rows + peers:
        pl.semaphore_signal(barrier, inc=1, device_id=device, device_id_type=MESH)
    pl.semaphore_wait(barrier, len(rows) + len(peers))

    tx, tp, tz = {}, {}, {}
    tx[0] = send(tokens_ref, acts.at[z, core, x], tx_send.at[0], tx_recv.at[0], across_x)
    tp[0, 0] = send(tokens_ref, acts.at[z, core, x], tp_send.at[0], tp_recv.at[0], partner)

    def offer(j):
        tz[j] = send(
            tokens_ref, acts.at[z, core, x], tz_send.at[j - 1], tz_recv.at[j - 1], peers[j - 1]
        )

    offer(2)
    swap = [
        send(src, dst, w_send.at[k], w_recv.at[k], partner)
        for k, (src, dst) in enumerate(weight_slices(ncore))
    ]

    unit_sums[...] = jnp.zeros_like(unit_sums)
    weight_parts[row] = jnp.zeros((16, 128), jnp.float32)
    small_send[...] = jnp.zeros_like(small_send)

    weight_copies = []

    def sum_weights():
        local[7].wait()
        ones_width = jnp.ones((8, width), jnp.bfloat16)
        for h in range(2):
            sums = dot_rows(ones_width, down[h * half : (h + 1) * half, :])
            for k in range(half // 128):
                line = slice(8 * h + k, 8 * h + k + 1)
                weight_parts[row, line, :] = sums[0:1, k * 128 : (k + 1) * 128]
        place = weight_parts.at[row]
        for k in range(3):
            weight_copies.append(send(place, place, ws_send.at[k], ws_recv.at[k], rows[k]))

    def total_weights():
        for copy in weight_copies:
            copy.wait_recv()
        total = weight_parts[0] + weight_parts[1] + weight_parts[2] + weight_parts[3]
        for h in range(2):
            sums = jnp.concatenate(
                [total[8 * h + k : 8 * h + k + 1, :] for k in range(half // 128)], axis=1
            )
            weight_terms[h] = three_terms(jnp.broadcast_to(sums, (8, half)))

    def arrive(j):
        tz[j].wait_recv()
        place = acts.at[zs[j], core, x]
        tx[j] = send(place, place, tx_send.at[j], tx_recv.at[j], across_x)
        tp[j, 0] = send(place, place, tp_send.at[2 * j], tp_recv.at[2 * j], partner)

    def arrive_across(j):
        tx[j].wait_recv()
        place = acts.at[zs[j], core, nx]
        tp[j, 1] = send(place, place, tp_send.at[2 * j + 1], tp_recv.at[2 * j + 1], partner)

    py, hp, hy, hf, mx, mz = {}, {}, {}, {}, {}, {}

    def ready(j):
        tp[j, 0].wait_recv()
        tp[j, 1].wait_recv()

    def columns_of(tile):
        return pl.ds(pl.multiple_of(tile * TILE, TILE), TILE)

    def both(ref, one, other):
        return jnp.concatenate([ref[one], ref[other]], axis=0)

    def multiply_block(b, tile, tiles):
        def body(t, carry):
            columns = columns_of(tile + t)
            product = dot(acts[z, 0, b], weights[0, :, columns]) + dot(
                acts[z, 1, b], weights[1, :, columns]
            )
            part_send[0, b, :, columns] = product.astype(jnp.bfloat16)
            return carry

        lax.fori_loop(0, tiles, body, 0, unroll=True)

    def multiply(j, tile, tiles, keep_both=False):
        def body(t, carry):
            columns = columns_of(tile + t)
            product = dot(both(acts.at[zs[j], 0], ny, y), weights[0, :, columns]) + dot(
                both(acts.at[zs[j], 1], ny, y), weights[1, :, columns]
            )
            if keep_both:
                part_wide[j, ny, :, columns] = product[:block]
            else:
                part_send[j, ny, :, columns] = product[:block].astype(jnp.bfloat16)
            part_wide[j, y, :, columns] = product[block:]
            return carry

        lax.fori_loop(0, tiles, body, 0, unroll=True)

    def send_part(n, j, b, place):
        py[n] = send(
            part_send.at[j, b, :, place],
            part_recv.at[j, b, :, place],
            py_send.at[n],
            py_recv.at[n],
            across_y,
        )

    def at_128(start, count):
        return pl.ds(pl.multiple_of(start, 128), count)

    def terms_of(n):
        if n < 2:
            return 0, [((x, nx)[n], y * wide, group, y * group)]
        if n == 2:
            return 0, [(y, last, left, wide)]
        j, p = divmod(n - 1, 2)
        if p == 0:
            return j, [(y, 0, group, 0)]
        return j, [(y, wide, group, group), (y, last, left, wide)]

    def hidden_place(n, who):
        if n < 2:
            return hidden.at[0, core, (x, nx)[n], :, at_128(who * group, group)]
        if n == 2:
            return hidden.at[0, core, who, :, wide:half]
        j, p = divmod(n - 1, 2)
        lanes = slice(0, group) if p == 0 else slice(group, half)
        return hidden.at[j, core, who, :, lanes]

    def activate(n):
        py[n].wait_recv()
        j, terms = terms_of(n)
        for b, column, count, unit in terms:
            gate, up = [
                part_wide[j, b, :, place] + part_recv[j, b, :, place].astype(jnp.float32)
                for place in (at_128(column, count), at_128(column + count, count))
            ]
            value = gate / (1.0 + jnp.exp(-gate)) * up
            hidden[j, core, b, :, at_128(unit, count)] = value.astype(jnp.bfloat16)
        place = hidden_place(n, y)
        hp[n] = send(place, place, hp_send.at[n], hp_recv.at[n], partner)

    def across(n):
        place = hidden_place(n, y)
        hy[n] = send(place, place, hy_send.at[n], hy_recv.at[n], across_y)

    def hand_over(n):
        hy[n].wait_recv()
        place = hidden_place(n, ny)
        hf[n] = send(place, place, hf_send.at[n], hf_recv.at[n], partner)

    def gate_and_up(j):
        ready(j)
        multiply(j, 0, wide // TILE)
        send_part(1 + 2 * j, j, ny, slice(0, wide))
        multiply(j, wide // TILE, (units - wide) // TILE)

    def send_rest(j):
        send_part(2 + 2 * j, j, ny, slice(wide, units))

    def strips_of(j):
        step = width // strips[j]
        return [
            (sum(strips[:j]) + q, slice(q * step, (q + 1) * step)) for q in range(strips[j])
        ]

    def send_across(j, n, place):
        mx[n] = send(
            out_send.at[j, nx, :, place],
            x_recv.at[j, :, place],
            mx_send.at[n],
            mx_recv.at[n],
            across_x,
        )

    def down_part(j, column_terms=False):
        for n in (1 + 2 * j, 2 + 2 * j):
            hp[n].wait_recv()
            hf[n].wait_recv()
        if column_terms:
            add_units(j)
            for h in range(2):
                unit_terms[h] = three_terms(unit_sums[h])

        def rows_of(h):
            chunk = both(hidden.at[j, h], nx, x)
            return jnp.concatenate([chunk, unit_terms[h]], axis=0) if column_terms else chunk

        def body(t, carry):
            columns = columns_of(t)
            product = dot(rows_of(0), down[0:half, columns]) + dot(
                rows_of(1), down[half:units, columns]
            )
            out_send[j, nx, :, columns] = product[:block].astype(jnp.bfloat16)
            out_wide[j, x, :, columns] = product[block : 2 * block]
            if column_terms:
                column_sums[:, columns] = jnp.sum(
                    product[2 * block :].reshape(2, 8, TILE), axis=0
                )
            return carry

        for n, place in strips_of(j):
            lax.fori_loop(place.start // TILE, place.stop // TILE, body, 0, unroll=True)
            send_across(j, n, place)

    def down_block(b, place):
        def body(t, carry):
            columns = columns_of(t)
            product = dot(hidden[0, 0, b], down[0:half, columns]) + dot(
                hidden[0, 1, b], down[half:units, columns]
            )
            out_wide[0, b, :, columns] = product
            out_send[0, b, :, columns] = product.astype(jnp.bfloat16)
            return carry

        lax.fori_loop(place.start // TILE, place.stop // TILE, body, 0, unroll=True)

    def down_across():
        for n in (1, 2):
            hp[n].wait_recv()
            hf[n].wait_recv()
        for n, place in strips_of(0):
            down_block(nx, place)
            send_across(0, n, place)

    def down_own():
        hp[0].wait_recv()
        hf[0].wait_recv()
        down_block(x, slice(0, width))

    def add_units(j):
        ones = jnp.ones((16, 2 * block), jnp.bfloat16)
        for h in range(2):
            unit_sums[h] += dot(ones, hidden[j, h].reshape(2 * block, half))

    def add_tokens(j):
        for b in range(2):
            terms = dot_rows(weight_terms[0], hidden[j, 0, b]) + dot_rows(
                weight_terms[1], hidden[j, 1, b]
            )
            small_send[j, b, 8:9, 0:block] = jnp.sum(terms, axis=0, keepdims=True)

    def checks(j):
        add_units(j)
        add_tokens(j)

    def add_across(j):
        for n, place in strips_of(j):
            mx[n].wait_recv()
            value = out_wide[j, x, :, place] + x_recv[j, :, place].astype(jnp.float32)
            if j == 0:
                own_sum[:, place] = value
            else:
                z_send[j - 1, :, place] = value.astype(jnp.bfloat16)
                mz[n] = send(
                    z_send.at[j - 1, :, place],
                    z_recv.at[j - 1, :, place],
                    mz_send.at[n - strips[0]],
                    mz_recv.at[n - strips[0]],
                    peers[j - 1],
                )

    def weights_here(p):
        for k in (2 * p, 2 * p + 1):
            local[1 + k].wait()
            swap[k].wait_recv()

    local[0].wait()
    tp[0, 0].wait_recv()
    weights_here(0)
    multiply_block(x, ny * (wide // TILE), wide // TILE)
    send_part(0, 0, x, at_128(ny * wide, wide))
    arrive_across(0)
    tp[0, 1].wait_recv()
    multiply_block(nx, ny * (wide // TILE), wide // TILE)
    send_part(1, 0, nx, at_128(ny * wide, wide))
    weights_here(1)
    multiply(0, last // TILE, 2 * left // TILE)
    send_part(2, 0, ny, slice(last, units))
    offer(3)
    weights_here(2)
    multiply(0, y * (wide // TILE), wide // TILE, keep_both=True)
    sum_weights()
    activate(0)
    across(0)
    arrive(2)
    offer(1)
    activate(1)
    across(1)
    activate(2)
    across(2)
    arrive_across(2)
    gate_and_up(2)
    send_rest(2)
    total_weights()
    hand_over(0)
    hand_over(1)
    hand_over(2)
    arrive(3)
    activate(5)
    across(5)
    arrive_across(3)
    gate_and_up(3)
    send_rest(3)
    arrive(1)
    activate(6)
    across(6)
    down_across()
    down_own()
    arrive_across(1)
    gate_and_up(1)
    activate(7)
    across(7)
    activate(8)
    across(8)
    send_rest(1)
    hand_over(5)
    hand_over(6)
    down_part(2)
    activate(3)
    across(3)
    checks(0)
    add_across(0)
    hand_over(7)
    hand_over(8)
    down_part(3)
    add_across(2)
    activate(4)
    across(4)
    checks(2)
    checks(3)
    add_across(3)
    hand_over(3)
    hand_over(4)
    down_part(1, column_terms=True)
    add_tokens(1)

    columns = jnp.sum(column_sums[...], axis=0, keepdims=True)
    for j in range(4):
        for b in range(2):
            for k in range(width // 128):
                small_send[j, b, k : k + 1, :] = columns[:, k * 128 : (k + 1) * 128]
    me = x * 4 + z
    small_recv[me] = small_send[0, x]
    small = [
        send(
            small_send.at[slot[0], slot[1]],
            small_recv.at[me],
            sm_send.at[k],
            sm_recv.at[k],
            peers[k],
        )
        for k, slot in enumerate(small_slots)
    ]
    add_across(1)
    for copy in small:
        copy.wait_recv()
    total = small_recv[0]
    for k in range(1, 8):
        total = total + small_recv[k]
    col_ref[...] = total[0:8] / math.sqrt(total_tokens)
    row_ref[...] = total[8:16] / math.sqrt(model_width)
    for j in range(1, 4):
        for n, _ in strips_of(j):
            mz[n].wait_recv()
    mixed_ref[...] = (
        own_sum[...]
        + z_recv[0].astype(jnp.float32)
        + z_recv[1].astype(jnp.float32)
        + z_recv[2].astype(jnp.float32)
    ).astype(jnp.bfloat16)
    for copy in sent:
        copy.wait_send()


def write_results(mixed_ref, col_ref, row_ref, mixed_out, col_out, row_out):
    mixed_out[...] = mixed_ref[...]
    for k in range(col_ref.shape[0]):
        col_out[pl.ds(k * 128, 128)] = col_ref[k]
    row_out[...] = row_ref[0, 0 : row_out.shape[0]]


def per_device_kernel(tokens, gate_up, down_weight):
    block, width = tokens.shape
    units = down_weight.shape[0]
    half = units // 2
    total_tokens = block * lax.axis_size(("dp", "col"))
    model_width = width * lax.axis_size("row")
    dma = pltpu.SemaphoreType.DMA
    bf16, f32 = jnp.bfloat16, jnp.float32
    sems = []
    for count in (6, 3, 4, 8, 9, 9, 9, 9, 10, 8, 3, 7):
        sems += [dma((count,)), dma((count,))]
    mixed, col, row = pl.pallas_call(
        functools.partial(kernel, total_tokens, model_width),
        out_shape=(
            jax.ShapeDtypeStruct((block, width), bf16),
            jax.ShapeDtypeStruct((8, 128), f32),
            jax.ShapeDtypeStruct((8, 128), f32),
        ),
        in_specs=[pl.BlockSpec(memory_space=pl.ANY)] * 3,
        out_specs=(pl.BlockSpec(memory_space=pltpu.VMEM),) * 3,
        scratch_shapes=[
            pltpu.VMEM((2, width, units), bf16),
            pltpu.VMEM((units, width), bf16),
            pltpu.VMEM((4, 2, 2, block, width), bf16),
            pltpu.VMEM((4, 2, block, units), f32),
            pltpu.VMEM((4, 2, block, units), bf16),
            pltpu.VMEM((4, 2, block, units), bf16),
            pltpu.VMEM((4, 2, 2, block, half), bf16),
            pltpu.VMEM((4, 2, block, width), f32),
            pltpu.VMEM((4, 2, block, width), bf16),
            pltpu.VMEM((4, block, width), bf16),
            pltpu.VMEM((3, block, width), bf16),
            pltpu.VMEM((3, block, width), bf16),
            pltpu.VMEM((block, width), f32),
            pltpu.VMEM((2, 16, half), f32),
            pltpu.VMEM((4, 16, 128), f32),
            pltpu.VMEM((2, 8, half), bf16),
            pltpu.VMEM((4, 2, 16, 128), f32),
            pltpu.VMEM((8, 16, 128), f32),
            pltpu.VMEM((2, 16, half), bf16),
            pltpu.VMEM((8, width), f32),
            dma((8,)),
        ]
        + sems,
        compiler_params=pltpu.CompilerParams(
            collective_id=0, has_side_effects=True, vmem_limit_bytes=56 * 2**20
        ),
        name="swiglu_grid",
    )(tokens, gate_up, down_weight)
    return pl.pallas_call(
        write_results,
        out_shape=(
            jax.ShapeDtypeStruct((block, width), bf16),
            jax.ShapeDtypeStruct((width,), f32),
            jax.ShapeDtypeStruct((block,), f32),
        ),
        name="write_results",
    )(mixed, col, row)


def fits_kernel(mesh):
    return dict(mesh.shape) == {"dp": 2, "row": 4, "col": 4}


def solution(mesh):
    body = per_device_kernel if fits_kernel(mesh) else per_device
    placed = (P(("dp", "col"), "row"), P(None, "row", ("dp", "col")), P(("dp", "col"), "row"))
    return jax.shard_map(
        body,
        mesh=mesh,
        in_specs=placed,
        out_specs=(P(("dp", "col"), "row"), P("row"), P(("dp", "col"))),
        check_vma=False,
    )
```

```python
import functools
import math

import jax
import jax.numpy as jnp
from jax import lax
from jax.experimental import pallas as pl
from jax.experimental.pallas import tpu as pltpu
from jax.sharding import PartitionSpec as P

MESH = pl.DeviceIdType.MESH
TILE = 256


def swiglu(partial_value):
    return (jax.nn.silu(partial_value[:, 0]) * partial_value[:, 1]).astype(jnp.bfloat16)


def hidden_units(partial_value):
    share = lax.psum_scatter(partial_value, "row", scatter_dimension=0, tiled=True)
    return lax.all_gather(swiglu(share), "row", axis=0, tiled=True)


def make_accumulate(hidden, shard_piece):
    columns_wide = hidden.astype(jnp.float32)
    piece_wide = shard_piece.astype(jnp.float32)
    output_part = jnp.dot(hidden, shard_piece, preferred_element_type=jnp.float32)
    column_part = jnp.dot(
        jnp.sum(columns_wide, axis=0), piece_wide, precision=lax.Precision.HIGHEST
    )
    row_part = jnp.dot(columns_wide, jnp.sum(piece_wide, axis=1), precision=lax.Precision.HIGHEST)
    return (output_part, column_part, row_part)


def per_device(tokens, gate_up, down_weight):
    total_tokens = tokens.shape[0] * lax.axis_size(("dp", "col"))
    model_width = tokens.shape[1] * lax.axis_size("row")
    group_rows = lax.all_gather(tokens, "col", axis=0, tiled=True)
    partial_value = jnp.einsum(
        "td,gdf->tgf",
        group_rows,
        lax.all_gather(gate_up, "dp", axis=2, tiled=True),
        preferred_element_type=jnp.float32,
    )
    hidden = hidden_units(partial_value)
    output_part, column_part, row_part = make_accumulate(
        hidden, lax.all_gather(down_weight, "dp", axis=0, tiled=True)
    )
    mixed, row_share = (
        lax.psum_scatter(output_part, "col", scatter_dimension=0, tiled=True),
        lax.psum_scatter(row_part, "col", scatter_dimension=0, tiled=True),
    )
    col_check = lax.psum(column_part, ("dp", "col")) / math.sqrt(total_tokens)
    row_check = lax.psum(row_share, "row") / math.sqrt(model_width)
    return (mixed.astype(jnp.bfloat16), col_check, row_check)


def dot(a, b):
    return jnp.dot(a, b, preferred_element_type=jnp.float32)


def dot_rows(a, b):
    return lax.dot_general(a, b, (((1,), (1,)), ((), ())), preferred_element_type=jnp.float32)


def three_terms(row):
    high = row.astype(jnp.bfloat16)
    rest = row - high.astype(jnp.float32)
    middle = rest.astype(jnp.bfloat16)
    low = (rest - middle.astype(jnp.float32)).astype(jnp.bfloat16)
    index = lax.broadcasted_iota(jnp.int32, row.shape, 0)
    terms = jnp.where(
        index == 0,
        high.astype(jnp.float32),
        jnp.where(
            index == 1,
            middle.astype(jnp.float32),
            jnp.where(index == 2, low.astype(jnp.float32), 0.0),
        ),
    )
    return terms.astype(jnp.bfloat16)


def kernel(
    total_tokens,
    model_width,
    tokens_ref,
    gate_up_ref,
    down_ref,
    mixed_ref,
    col_ref,
    row_ref,
    weights,
    down,
    acts,
    part_wide,
    part_send,
    part_recv,
    hidden,
    out_wide,
    out_send,
    x_recv,
    z_send,
    z_recv,
    own_sum,
    unit_sums,
    weight_parts,
    weight_terms,
    small_send,
    small_recv,
    unit_terms,
    column_sums,
    local_sem,
    w_send,
    w_recv,
    tz_send,
    tz_recv,
    tx_send,
    tx_recv,
    tp_send,
    tp_recv,
    py_send,
    py_recv,
    hp_send,
    hp_recv,
    hy_send,
    hy_recv,
    hf_send,
    hf_recv,
    mx_send,
    mx_recv,
    mz_send,
    mz_recv,
    ws_send,
    ws_recv,
    sm_send,
    sm_recv,
):
    block, width = tokens_ref.shape
    units = down_ref.shape[0]
    half = units // 2
    group = half // 256 * 128
    left = half - 2 * group
    wide, last = 2 * group, 4 * group
    strips = (2, 4, 2, 2)
    x = lax.axis_index("dp")
    row = lax.axis_index("row")
    z = lax.axis_index("col")
    y, core = lax.div(row, 2), lax.rem(row, 2)
    nx, ny, ncore = 1 - x, 1 - y, 1 - core
    zs = [z, z + 1 - 2 * lax.rem(z, 2), lax.rem(z + 2, 4), 3 - z]
    partner = (x, y * 2 + ncore, z)
    across_y = (x, ny * 2 + core, z)
    across_x = (nx, row, z)
    rows = [(x, lax.rem(row + k, 4), z) for k in range(1, 4)]
    peers = [(x, row, zs[j]) for j in range(1, 4)] + [(nx, row, zs[j]) for j in range(4)]
    small_slots = [(j, x) for j in range(1, 4)] + [(j, nx) for j in range(4)]
    sent = []

    def send(src, dst, send_sem, recv_sem, device):
        copy = pltpu.make_async_remote_copy(
            src_ref=src,
            dst_ref=dst,
            send_sem=send_sem,
            recv_sem=recv_sem,
            device_id=device,
            device_id_type=MESH,
        )
        copy.start()
        sent.append(copy)
        return copy

    def weight_slices(which):
        for start, count in ((ny * group, group), (2 * group, left), (y * group, group)):
            for g in range(2):
                lanes = pl.ds(pl.multiple_of(which * half + start, 128), count)
                place = pl.ds(pl.multiple_of(2 * start + g * count, 128), count)
                yield gate_up_ref.at[g, :, lanes], weights.at[core, :, place]

    local = [pltpu.make_async_copy(tokens_ref, acts.at[z, core, x], local_sem.at[0])]
    for k, (src, dst) in enumerate(weight_slices(core)):
        local.append(pltpu.make_async_copy(src, dst, local_sem.at[1 + k]))
    local.append(pltpu.make_async_copy(down_ref, down, local_sem.at[7]))
    for copy in local:
        copy.start()

    barrier = pltpu.get_barrier_semaphore()
    for device in rows + peers:
        pl.semaphore_signal(barrier, inc=1, device_id=device, device_id_type=MESH)
    pl.semaphore_wait(barrier, len(rows) + len(peers))

    tx, tp, tz = {}, {}, {}
    tx[0] = send(tokens_ref, acts.at[z, core, x], tx_send.at[0], tx_recv.at[0], across_x)
    tp[0, 0] = send(tokens_ref, acts.at[z, core, x], tp_send.at[0], tp_recv.at[0], partner)

    def offer(j):
        tz[j] = send(
            tokens_ref, acts.at[z, core, x], tz_send.at[j - 1], tz_recv.at[j - 1], peers[j - 1]
        )

    offer(1)
    swap = [
        send(src, dst, w_send.at[k], w_recv.at[k], partner)
        for k, (src, dst) in enumerate(weight_slices(ncore))
    ]

    unit_sums[...] = jnp.zeros_like(unit_sums)
    weight_parts[row] = jnp.zeros((16, 128), jnp.float32)
    small_send[...] = jnp.zeros_like(small_send)

    weight_copies = []

    def sum_weights():
        local[7].wait()
        ones_width = jnp.ones((8, width), jnp.bfloat16)
        for h in range(2):
            sums = dot_rows(ones_width, down[h * half : (h + 1) * half, :])
            for k in range(half // 128):
                line = slice(8 * h + k, 8 * h + k + 1)
                weight_parts[row, line, :] = sums[0:1, k * 128 : (k + 1) * 128]
        place = weight_parts.at[row]
        for k in range(3):
            weight_copies.append(send(place, place, ws_send.at[k], ws_recv.at[k], rows[k]))

    def total_weights():
        for copy in weight_copies:
            copy.wait_recv()
        total = weight_parts[0] + weight_parts[1] + weight_parts[2] + weight_parts[3]
        for h in range(2):
            sums = jnp.concatenate(
                [total[8 * h + k : 8 * h + k + 1, :] for k in range(half // 128)], axis=1
            )
            weight_terms[h] = three_terms(jnp.broadcast_to(sums, (8, half)))

    def arrive(j):
        tz[j].wait_recv()
        place = acts.at[zs[j], core, x]
        tx[j] = send(place, place, tx_send.at[j], tx_recv.at[j], across_x)
        tp[j, 0] = send(place, place, tp_send.at[2 * j], tp_recv.at[2 * j], partner)

    def arrive_across(j):
        tx[j].wait_recv()
        place = acts.at[zs[j], core, nx]
        tp[j, 1] = send(place, place, tp_send.at[2 * j + 1], tp_recv.at[2 * j + 1], partner)

    py, hp, hy, hf, mx, mz = {}, {}, {}, {}, {}, {}

    def ready(j):
        tp[j, 0].wait_recv()
        tp[j, 1].wait_recv()

    def columns_of(tile):
        return pl.ds(pl.multiple_of(tile * TILE, TILE), TILE)

    def both(ref, one, other):
        return jnp.concatenate([ref[one], ref[other]], axis=0)

    def multiply_block(b, tile, tiles):
        def body(t, carry):
            columns = columns_of(tile + t)
            product = dot(acts[z, 0, b], weights[0, :, columns]) + dot(
                acts[z, 1, b], weights[1, :, columns]
            )
            part_send[0, b, :, columns] = product.astype(jnp.bfloat16)
            return carry

        lax.fori_loop(0, tiles, body, 0, unroll=True)

    def multiply(j, tile, tiles, keep_both=False):
        def body(t, carry):
            columns = columns_of(tile + t)
            product = dot(both(acts.at[zs[j], 0], ny, y), weights[0, :, columns]) + dot(
                both(acts.at[zs[j], 1], ny, y), weights[1, :, columns]
            )
            if keep_both:
                part_wide[j, ny, :, columns] = product[:block]
            else:
                part_send[j, ny, :, columns] = product[:block].astype(jnp.bfloat16)
            part_wide[j, y, :, columns] = product[block:]
            return carry

        lax.fori_loop(0, tiles, body, 0, unroll=True)

    def send_part(n, j, b, place):
        py[n] = send(
            part_send.at[j, b, :, place],
            part_recv.at[j, b, :, place],
            py_send.at[n],
            py_recv.at[n],
            across_y,
        )

    def at_128(start, count):
        return pl.ds(pl.multiple_of(start, 128), count)

    def terms_of(n):
        if n < 2:
            return 0, [((x, nx)[n], y * wide, group, y * group)]
        if n == 2:
            return 0, [(y, last, left, wide)]
        j, p = divmod(n - 1, 2)
        if p == 0:
            return j, [(y, 0, group, 0)]
        return j, [(y, wide, group, group), (y, last, left, wide)]

    def hidden_place(n, who):
        if n < 2:
            return hidden.at[0, core, (x, nx)[n], :, at_128(who * group, group)]
        if n == 2:
            return hidden.at[0, core, who, :, wide:half]
        j, p = divmod(n - 1, 2)
        lanes = slice(0, group) if p == 0 else slice(group, half)
        return hidden.at[j, core, who, :, lanes]

    def activate(n):
        py[n].wait_recv()
        j, terms = terms_of(n)
        for b, column, count, unit in terms:
            gate, up = [
                part_wide[j, b, :, place] + part_recv[j, b, :, place].astype(jnp.float32)
                for place in (at_128(column, count), at_128(column + count, count))
            ]
            value = gate / (1.0 + jnp.exp(-gate)) * up
            hidden[j, core, b, :, at_128(unit, count)] = value.astype(jnp.bfloat16)
        place = hidden_place(n, y)
        hp[n] = send(place, place, hp_send.at[n], hp_recv.at[n], partner)

    def across(n):
        place = hidden_place(n, y)
        hy[n] = send(place, place, hy_send.at[n], hy_recv.at[n], across_y)

    def hand_over(n):
        hy[n].wait_recv()
        place = hidden_place(n, ny)
        hf[n] = send(place, place, hf_send.at[n], hf_recv.at[n], partner)

    def first_part(j):
        multiply(j, 0, wide // TILE)
        send_part(1 + 2 * j, j, ny, slice(0, wide))

    def rest_part(j):
        multiply(j, wide // TILE, (units - wide) // TILE)

    def send_rest(j):
        send_part(2 + 2 * j, j, ny, slice(wide, units))

    def strips_of(j):
        step = width // strips[j]
        return [
            (sum(strips[:j]) + q, slice(q * step, (q + 1) * step)) for q in range(strips[j])
        ]

    def send_across(j, n, place):
        mx[n] = send(
            out_send.at[j, nx, :, place],
            x_recv.at[j, :, place],
            mx_send.at[n],
            mx_recv.at[n],
            across_x,
        )

    def down_part(j):
        for n in (1 + 2 * j, 2 + 2 * j):
            hp[n].wait_recv()
            hf[n].wait_recv()

        def body(t, carry):
            columns = columns_of(t)
            product = dot(both(hidden.at[j, 0], nx, x), down[0:half, columns]) + dot(
                both(hidden.at[j, 1], nx, x), down[half:units, columns]
            )
            out_send[j, nx, :, columns] = product[:block].astype(jnp.bfloat16)
            out_wide[j, x, :, columns] = product[block:]
            return carry

        for n, place in strips_of(j):
            lax.fori_loop(place.start // TILE, place.stop // TILE, body, 0, unroll=True)
            send_across(j, n, place)

    def down_across():
        for n in (1, 2):
            hp[n].wait_recv()
            hf[n].wait_recv()

        def body(t, carry):
            columns = columns_of(t)
            product = dot(hidden[0, 0, nx], down[0:half, columns]) + dot(
                hidden[0, 1, nx], down[half:units, columns]
            )
            out_send[0, nx, :, columns] = product.astype(jnp.bfloat16)
            return carry

        for n, place in strips_of(0):
            lax.fori_loop(place.start // TILE, place.stop // TILE, body, 0, unroll=True)
            send_across(0, n, place)

    def down_own():
        hp[0].wait_recv()
        hf[0].wait_recv()
        add_units(0)
        for h in range(2):
            unit_terms[h] = three_terms(unit_sums[h])

        def rows_of(h):
            return jnp.concatenate([hidden[0, h, x], unit_terms[h]], axis=0)

        def body(t, carry):
            columns = columns_of(t)
            product = dot(rows_of(0), down[0:half, columns]) + dot(
                rows_of(1), down[half:units, columns]
            )
            out_wide[0, x, :, columns] = product[:block]
            column_sums[:, columns] = jnp.sum(product[block:].reshape(2, 8, TILE), axis=0)
            return carry

        lax.fori_loop(0, width // TILE, body, 0, unroll=True)

    def add_units(j):
        ones = jnp.ones((16, 2 * block), jnp.bfloat16)
        for h in range(2):
            unit_sums[h] += dot(ones, hidden[j, h].reshape(2 * block, half))

    def add_tokens(j):
        for b in range(2):
            terms = dot_rows(weight_terms[0], hidden[j, 0, b]) + dot_rows(
                weight_terms[1], hidden[j, 1, b]
            )
            small_send[j, b, 8:9, 0:block] = jnp.sum(terms, axis=0, keepdims=True)

    def checks(j):
        add_units(j)
        add_tokens(j)

    def add_across(j):
        for n, place in strips_of(j):
            mx[n].wait_recv()
            value = out_wide[j, x, :, place] + x_recv[j, :, place].astype(jnp.float32)
            if j == 0:
                own_sum[:, place] = value
            else:
                z_send[j - 1, :, place] = value.astype(jnp.bfloat16)
                mz[n] = send(
                    z_send.at[j - 1, :, place],
                    z_recv.at[j - 1, :, place],
                    mz_send.at[n - strips[0]],
                    mz_recv.at[n - strips[0]],
                    peers[j - 1],
                )

    def weights_here(p):
        for k in (2 * p, 2 * p + 1):
            local[1 + k].wait()
            swap[k].wait_recv()

    local[0].wait()
    tp[0, 0].wait_recv()
    weights_here(0)
    multiply_block(x, ny * (wide // TILE), wide // TILE)
    send_part(0, 0, x, at_128(ny * wide, wide))
    offer(2)
    arrive_across(0)
    arrive(1)
    tp[0, 1].wait_recv()
    multiply_block(nx, ny * (wide // TILE), wide // TILE)
    send_part(1, 0, nx, at_128(ny * wide, wide))
    weights_here(1)
    multiply(0, last // TILE, 2 * left // TILE)
    send_part(2, 0, ny, slice(last, units))
    weights_here(2)
    multiply(0, y * (wide // TILE), wide // TILE, keep_both=True)
    sum_weights()
    activate(0)
    offer(3)
    arrive_across(1)
    ready(1)
    first_part(1)
    activate(1)
    across(1)
    arrive(2)
    activate(2)
    rest_part(1)
    total_weights()
    arrive_across(2)
    ready(2)
    first_part(2)
    rest_part(2)
    send_rest(2)
    hand_over(1)
    arrive(3)
    activate(3)
    activate(5)
    across(5)
    arrive_across(3)
    ready(3)
    first_part(3)
    rest_part(3)
    send_rest(3)
    activate(6)
    across(6)
    activate(7)
    across(7)
    hand_over(5)
    activate(8)
    across(8)
    send_rest(1)
    across(3)
    hand_over(6)
    down_part(2)
    checks(2)
    hand_over(7)
    hand_over(8)
    down_part(3)
    add_across(2)
    activate(4)
    across(4)
    across(2)
    across(0)
    checks(3)
    add_across(3)
    hand_over(3)
    hand_over(4)
    down_part(1)
    hand_over(2)
    down_across()
    checks(1)
    hand_over(0)
    down_own()
    add_tokens(0)

    columns = jnp.sum(column_sums[...], axis=0, keepdims=True)
    for j in range(4):
        for b in range(2):
            for k in range(width // 128):
                small_send[j, b, k : k + 1, :] = columns[:, k * 128 : (k + 1) * 128]
    me = x * 4 + z
    small_recv[me] = small_send[0, x]
    small = [
        send(
            small_send.at[slot[0], slot[1]],
            small_recv.at[me],
            sm_send.at[k],
            sm_recv.at[k],
            peers[k],
        )
        for k, slot in enumerate(small_slots)
    ]
    add_across(1)
    add_across(0)
    for copy in small:
        copy.wait_recv()
    total = small_recv[0]
    for k in range(1, 8):
        total = total + small_recv[k]
    col_ref[...] = total[0:8] / math.sqrt(total_tokens)
    row_ref[...] = total[8:16] / math.sqrt(model_width)
    for j in range(1, 4):
        for n, _ in strips_of(j):
            mz[n].wait_recv()
    mixed_ref[...] = (
        own_sum[...]
        + z_recv[0].astype(jnp.float32)
        + z_recv[1].astype(jnp.float32)
        + z_recv[2].astype(jnp.float32)
    ).astype(jnp.bfloat16)
    for copy in sent:
        copy.wait_send()


def write_results(mixed_ref, col_ref, row_ref, mixed_out, col_out, row_out):
    mixed_out[...] = mixed_ref[...]
    for k in range(col_ref.shape[0]):
        col_out[pl.ds(k * 128, 128)] = col_ref[k]
    row_out[...] = row_ref[0, 0 : row_out.shape[0]]


def per_device_kernel(tokens, gate_up, down_weight):
    block, width = tokens.shape
    units = down_weight.shape[0]
    half = units // 2
    total_tokens = block * lax.axis_size(("dp", "col"))
    model_width = width * lax.axis_size("row")
    dma = pltpu.SemaphoreType.DMA
    bf16, f32 = jnp.bfloat16, jnp.float32
    sems = []
    for count in (6, 3, 4, 8, 9, 9, 9, 9, 10, 8, 3, 7):
        sems += [dma((count,)), dma((count,))]
    mixed, col, row = pl.pallas_call(
        functools.partial(kernel, total_tokens, model_width),
        out_shape=(
            jax.ShapeDtypeStruct((block, width), bf16),
            jax.ShapeDtypeStruct((8, 128), f32),
            jax.ShapeDtypeStruct((8, 128), f32),
        ),
        in_specs=[pl.BlockSpec(memory_space=pl.ANY)] * 3,
        out_specs=(pl.BlockSpec(memory_space=pltpu.VMEM),) * 3,
        scratch_shapes=[
            pltpu.VMEM((2, width, units), bf16),
            pltpu.VMEM((units, width), bf16),
            pltpu.VMEM((4, 2, 2, block, width), bf16),
            pltpu.VMEM((4, 2, block, units), f32),
            pltpu.VMEM((4, 2, block, units), bf16),
            pltpu.VMEM((4, 2, block, units), bf16),
            pltpu.VMEM((4, 2, 2, block, half), bf16),
            pltpu.VMEM((4, 2, block, width), f32),
            pltpu.VMEM((4, 2, block, width), bf16),
            pltpu.VMEM((4, block, width), bf16),
            pltpu.VMEM((3, block, width), bf16),
            pltpu.VMEM((3, block, width), bf16),
            pltpu.VMEM((block, width), f32),
            pltpu.VMEM((2, 16, half), f32),
            pltpu.VMEM((4, 16, 128), f32),
            pltpu.VMEM((2, 8, half), bf16),
            pltpu.VMEM((4, 2, 16, 128), f32),
            pltpu.VMEM((8, 16, 128), f32),
            pltpu.VMEM((2, 16, half), bf16),
            pltpu.VMEM((8, width), f32),
            dma((8,)),
        ]
        + sems,
        compiler_params=pltpu.CompilerParams(
            collective_id=0, has_side_effects=True, vmem_limit_bytes=56 * 2**20
        ),
        name="swiglu_grid",
    )(tokens, gate_up, down_weight)
    return pl.pallas_call(
        write_results,
        out_shape=(
            jax.ShapeDtypeStruct((block, width), bf16),
            jax.ShapeDtypeStruct((width,), f32),
            jax.ShapeDtypeStruct((block,), f32),
        ),
        name="write_results",
    )(mixed, col, row)


def fits_kernel(mesh):
    return dict(mesh.shape) == {"dp": 2, "row": 4, "col": 4}


def solution(mesh):
    body = per_device_kernel if fits_kernel(mesh) else per_device
    placed = (P(("dp", "col"), "row"), P(None, "row", ("dp", "col")), P(("dp", "col"), "row"))
    return jax.shard_map(
        body,
        mesh=mesh,
        in_specs=placed,
        out_specs=(P(("dp", "col"), "row"), P("row"), P(("dp", "col"))),
        check_vma=False,
    )
```

```python
import functools
import math

import jax
import jax.numpy as jnp
from jax import lax
from jax.experimental import pallas as pl
from jax.experimental.pallas import tpu as pltpu
from jax.sharding import PartitionSpec as P

MESH = pl.DeviceIdType.MESH
TILE = 256


def swiglu(partial_value):
    return (jax.nn.silu(partial_value[:, 0]) * partial_value[:, 1]).astype(jnp.bfloat16)


def hidden_units(partial_value):
    share = lax.psum_scatter(partial_value, "row", scatter_dimension=0, tiled=True)
    return lax.all_gather(swiglu(share), "row", axis=0, tiled=True)


def make_accumulate(hidden, shard_piece):
    columns_wide = hidden.astype(jnp.float32)
    piece_wide = shard_piece.astype(jnp.float32)
    output_part = jnp.dot(hidden, shard_piece, preferred_element_type=jnp.float32)
    column_part = jnp.dot(
        jnp.sum(columns_wide, axis=0), piece_wide, precision=lax.Precision.HIGHEST
    )
    row_part = jnp.dot(columns_wide, jnp.sum(piece_wide, axis=1), precision=lax.Precision.HIGHEST)
    return (output_part, column_part, row_part)


def per_device(tokens, gate_up, down_weight):
    total_tokens = tokens.shape[0] * lax.axis_size(("dp", "col"))
    model_width = tokens.shape[1] * lax.axis_size("row")
    group_rows = lax.all_gather(tokens, "col", axis=0, tiled=True)
    partial_value = jnp.einsum(
        "td,gdf->tgf",
        group_rows,
        lax.all_gather(gate_up, "dp", axis=2, tiled=True),
        preferred_element_type=jnp.float32,
    )
    hidden = hidden_units(partial_value)
    output_part, column_part, row_part = make_accumulate(
        hidden, lax.all_gather(down_weight, "dp", axis=0, tiled=True)
    )
    mixed, row_share = (
        lax.psum_scatter(output_part, "col", scatter_dimension=0, tiled=True),
        lax.psum_scatter(row_part, "col", scatter_dimension=0, tiled=True),
    )
    col_check = lax.psum(column_part, ("dp", "col")) / math.sqrt(total_tokens)
    row_check = lax.psum(row_share, "row") / math.sqrt(model_width)
    return (mixed.astype(jnp.bfloat16), col_check, row_check)


def dot(a, b):
    return jnp.dot(a, b, preferred_element_type=jnp.float32)


def dot_rows(a, b):
    return lax.dot_general(a, b, (((1,), (1,)), ((), ())), preferred_element_type=jnp.float32)


def three_terms(row):
    high = row.astype(jnp.bfloat16)
    rest = row - high.astype(jnp.float32)
    middle = rest.astype(jnp.bfloat16)
    low = (rest - middle.astype(jnp.float32)).astype(jnp.bfloat16)
    index = lax.broadcasted_iota(jnp.int32, row.shape, 0)
    terms = jnp.where(
        index == 0,
        high.astype(jnp.float32),
        jnp.where(
            index == 1,
            middle.astype(jnp.float32),
            jnp.where(index == 2, low.astype(jnp.float32), 0.0),
        ),
    )
    return terms.astype(jnp.bfloat16)


def kernel(
    total_tokens,
    model_width,
    tokens_ref,
    gate_up_ref,
    down_ref,
    mixed_ref,
    col_ref,
    row_ref,
    weights,
    down,
    acts,
    part_wide,
    part_send,
    part_recv,
    hidden,
    out_wide,
    out_send,
    x_recv,
    z_send,
    z_recv,
    own_sum,
    unit_sums,
    weight_parts,
    weight_terms,
    small_send,
    small_recv,
    unit_terms,
    column_sums,
    local_sem,
    w_send,
    w_recv,
    tz_send,
    tz_recv,
    tx_send,
    tx_recv,
    tp_send,
    tp_recv,
    py_send,
    py_recv,
    hp_send,
    hp_recv,
    hy_send,
    hy_recv,
    hf_send,
    hf_recv,
    mx_send,
    mx_recv,
    mz_send,
    mz_recv,
    ws_send,
    ws_recv,
    sm_send,
    sm_recv,
):
    block, width = tokens_ref.shape
    units = down_ref.shape[0]
    half = units // 2
    group = half // 256 * 128
    left = half - 2 * group
    wide, last = 2 * group, 4 * group
    strips = (2, 4, 2, 4)
    x = lax.axis_index("dp")
    row = lax.axis_index("row")
    z = lax.axis_index("col")
    y, core = lax.div(row, 2), lax.rem(row, 2)
    nx, ny, ncore = 1 - x, 1 - y, 1 - core
    zs = [z, z + 1 - 2 * lax.rem(z, 2), lax.rem(z + 2, 4), 3 - z]
    partner = (x, y * 2 + ncore, z)
    across_y = (x, ny * 2 + core, z)
    across_x = (nx, row, z)
    rows = [(x, lax.rem(row + k, 4), z) for k in range(1, 4)]
    peers = [(x, row, zs[j]) for j in range(1, 4)] + [(nx, row, zs[j]) for j in range(4)]
    small_slots = [(j, x) for j in range(1, 4)] + [(j, nx) for j in range(4)]
    sent = []

    def send(src, dst, send_sem, recv_sem, device):
        copy = pltpu.make_async_remote_copy(
            src_ref=src,
            dst_ref=dst,
            send_sem=send_sem,
            recv_sem=recv_sem,
            device_id=device,
            device_id_type=MESH,
        )
        copy.start()
        sent.append(copy)
        return copy

    def weight_slices(which):
        for start, count in ((ny * group, group), (2 * group, left), (y * group, group)):
            for g in range(2):
                lanes = pl.ds(pl.multiple_of(which * half + start, 128), count)
                place = pl.ds(pl.multiple_of(2 * start + g * count, 128), count)
                yield gate_up_ref.at[g, :, lanes], weights.at[core, :, place]

    local = [pltpu.make_async_copy(tokens_ref, acts.at[z, core, x], local_sem.at[0])]
    for k, (src, dst) in enumerate(weight_slices(core)):
        local.append(pltpu.make_async_copy(src, dst, local_sem.at[1 + k]))
    local.append(pltpu.make_async_copy(down_ref, down, local_sem.at[7]))
    for copy in local:
        copy.start()

    barrier = pltpu.get_barrier_semaphore()
    for device in rows + peers:
        pl.semaphore_signal(barrier, inc=1, device_id=device, device_id_type=MESH)
    pl.semaphore_wait(barrier, len(rows) + len(peers))

    tx, tp, tz = {}, {}, {}
    tx[0] = send(tokens_ref, acts.at[z, core, x], tx_send.at[0], tx_recv.at[0], across_x)
    tp[0, 0] = send(tokens_ref, acts.at[z, core, x], tp_send.at[0], tp_recv.at[0], partner)

    def offer(j):
        tz[j] = send(
            tokens_ref, acts.at[z, core, x], tz_send.at[j - 1], tz_recv.at[j - 1], peers[j - 1]
        )

    offer(2)
    swap = [
        send(src, dst, w_send.at[k], w_recv.at[k], partner)
        for k, (src, dst) in enumerate(weight_slices(ncore))
    ]

    unit_sums[...] = jnp.zeros_like(unit_sums)
    weight_parts[row] = jnp.zeros((16, 128), jnp.float32)
    small_send[...] = jnp.zeros_like(small_send)

    weight_copies = []

    def sum_weights():
        local[7].wait()
        ones_width = jnp.ones((8, width), jnp.bfloat16)
        for h in range(2):
            sums = dot_rows(ones_width, down[h * half : (h + 1) * half, :])
            for k in range(half // 128):
                line = slice(8 * h + k, 8 * h + k + 1)
                weight_parts[row, line, :] = sums[0:1, k * 128 : (k + 1) * 128]
        place = weight_parts.at[row]
        for k in range(3):
            weight_copies.append(send(place, place, ws_send.at[k], ws_recv.at[k], rows[k]))

    def total_weights():
        for copy in weight_copies:
            copy.wait_recv()
        total = weight_parts[0] + weight_parts[1] + weight_parts[2] + weight_parts[3]
        for h in range(2):
            sums = jnp.concatenate(
                [total[8 * h + k : 8 * h + k + 1, :] for k in range(half // 128)], axis=1
            )
            weight_terms[h] = three_terms(jnp.broadcast_to(sums, (8, half)))

    def arrive(j):
        tz[j].wait_recv()
        place = acts.at[zs[j], core, x]
        tx[j] = send(place, place, tx_send.at[j], tx_recv.at[j], across_x)
        tp[j, 0] = send(place, place, tp_send.at[2 * j], tp_recv.at[2 * j], partner)

    def arrive_across(j):
        tx[j].wait_recv()
        place = acts.at[zs[j], core, nx]
        tp[j, 1] = send(place, place, tp_send.at[2 * j + 1], tp_recv.at[2 * j + 1], partner)

    py, hp, hy, hf, mx, mz = {}, {}, {}, {}, {}, {}

    def ready(j):
        tp[j, 0].wait_recv()
        tp[j, 1].wait_recv()

    def columns_of(tile):
        return pl.ds(pl.multiple_of(tile * TILE, TILE), TILE)

    def both(ref, one, other):
        return jnp.concatenate([ref[one], ref[other]], axis=0)

    def multiply_block(b, tile, tiles):
        def body(t, carry):
            columns = columns_of(tile + t)
            product = dot(acts[z, 0, b], weights[0, :, columns]) + dot(
                acts[z, 1, b], weights[1, :, columns]
            )
            part_send[0, b, :, columns] = product.astype(jnp.bfloat16)
            return carry

        lax.fori_loop(0, tiles, body, 0, unroll=True)

    def multiply(j, tile, tiles, keep_both=False):
        def body(t, carry):
            columns = columns_of(tile + t)
            product = dot(both(acts.at[zs[j], 0], ny, y), weights[0, :, columns]) + dot(
                both(acts.at[zs[j], 1], ny, y), weights[1, :, columns]
            )
            if keep_both:
                part_wide[j, ny, :, columns] = product[:block]
            else:
                part_send[j, ny, :, columns] = product[:block].astype(jnp.bfloat16)
            part_wide[j, y, :, columns] = product[block:]
            return carry

        lax.fori_loop(0, tiles, body, 0, unroll=True)

    def send_part(n, j, b, place):
        py[n] = send(
            part_send.at[j, b, :, place],
            part_recv.at[j, b, :, place],
            py_send.at[n],
            py_recv.at[n],
            across_y,
        )

    def at_128(start, count):
        return pl.ds(pl.multiple_of(start, 128), count)

    def terms_of(n):
        if n < 2:
            return 0, [((x, nx)[n], y * wide, group, y * group)]
        if n == 2:
            return 0, [(y, last, left, wide)]
        j, p = divmod(n - 1, 2)
        if p == 0:
            return j, [(y, 0, group, 0)]
        return j, [(y, wide, group, group), (y, last, left, wide)]

    def hidden_place(n, who):
        if n < 2:
            return hidden.at[0, core, (x, nx)[n], :, at_128(who * group, group)]
        if n == 2:
            return hidden.at[0, core, who, :, wide:half]
        j, p = divmod(n - 1, 2)
        lanes = slice(0, group) if p == 0 else slice(group, half)
        return hidden.at[j, core, who, :, lanes]

    def activate(n):
        py[n].wait_recv()
        j, terms = terms_of(n)
        for b, column, count, unit in terms:
            gate, up = [
                part_wide[j, b, :, place] + part_recv[j, b, :, place].astype(jnp.float32)
                for place in (at_128(column, count), at_128(column + count, count))
            ]
            value = gate / (1.0 + jnp.exp(-gate)) * up
            hidden[j, core, b, :, at_128(unit, count)] = value.astype(jnp.bfloat16)
        place = hidden_place(n, y)
        hp[n] = send(place, place, hp_send.at[n], hp_recv.at[n], partner)

    def across(n):
        place = hidden_place(n, y)
        hy[n] = send(place, place, hy_send.at[n], hy_recv.at[n], across_y)

    def hand_over(n):
        hy[n].wait_recv()
        place = hidden_place(n, ny)
        hf[n] = send(place, place, hf_send.at[n], hf_recv.at[n], partner)

    def gate_and_up(j):
        ready(j)
        multiply(j, 0, wide // TILE)
        send_part(1 + 2 * j, j, ny, slice(0, wide))
        multiply(j, wide // TILE, (units - wide) // TILE)

    def send_rest(j):
        send_part(2 + 2 * j, j, ny, slice(wide, units))

    def strips_of(j):
        step = width // strips[j]
        return [
            (sum(strips[:j]) + q, slice(q * step, (q + 1) * step)) for q in range(strips[j])
        ]

    def send_across(j, n, place):
        mx[n] = send(
            out_send.at[j, nx, :, place],
            x_recv.at[j, :, place],
            mx_send.at[n],
            mx_recv.at[n],
            across_x,
        )

    def down_part(j, column_terms=False):
        for n in (1 + 2 * j, 2 + 2 * j):
            hp[n].wait_recv()
            hf[n].wait_recv()
        if column_terms:
            add_units(j)
            for h in range(2):
                unit_terms[h] = three_terms(unit_sums[h])

        def rows_of(h):
            chunk = both(hidden.at[j, h], nx, x)
            return jnp.concatenate([chunk, unit_terms[h]], axis=0) if column_terms else chunk

        def body(t, carry):
            columns = columns_of(t)
            product = dot(rows_of(0), down[0:half, columns]) + dot(
                rows_of(1), down[half:units, columns]
            )
            out_send[j, nx, :, columns] = product[:block].astype(jnp.bfloat16)
            out_wide[j, x, :, columns] = product[block : 2 * block]
            if column_terms:
                column_sums[:, columns] = jnp.sum(
                    product[2 * block :].reshape(2, 8, TILE), axis=0
                )
            return carry

        for n, place in strips_of(j):
            lax.fori_loop(place.start // TILE, place.stop // TILE, body, 0, unroll=True)
            send_across(j, n, place)

    def down_block(b, place):
        def body(t, carry):
            columns = columns_of(t)
            product = dot(hidden[0, 0, b], down[0:half, columns]) + dot(
                hidden[0, 1, b], down[half:units, columns]
            )
            out_wide[0, b, :, columns] = product
            out_send[0, b, :, columns] = product.astype(jnp.bfloat16)
            return carry

        lax.fori_loop(place.start // TILE, place.stop // TILE, body, 0, unroll=True)

    def down_across():
        for n in (1, 2):
            hp[n].wait_recv()
            hf[n].wait_recv()
        for n, place in strips_of(0):
            down_block(nx, place)
            send_across(0, n, place)

    def down_own():
        hp[0].wait_recv()
        hf[0].wait_recv()
        down_block(x, slice(0, width))

    def add_units(j):
        ones = jnp.ones((16, 2 * block), jnp.bfloat16)
        for h in range(2):
            unit_sums[h] += dot(ones, hidden[j, h].reshape(2 * block, half))

    def add_tokens(j):
        for b in range(2):
            terms = dot_rows(weight_terms[0], hidden[j, 0, b]) + dot_rows(
                weight_terms[1], hidden[j, 1, b]
            )
            small_send[j, b, 8:9, 0:block] = jnp.sum(terms, axis=0, keepdims=True)

    def checks(j):
        add_units(j)
        add_tokens(j)

    def add_across(j):
        for n, place in strips_of(j):
            mx[n].wait_recv()
            value = out_wide[j, x, :, place] + x_recv[j, :, place].astype(jnp.float32)
            if j == 0:
                own_sum[:, place] = value
            else:
                z_send[j - 1, :, place] = value.astype(jnp.bfloat16)
                mz[n] = send(
                    z_send.at[j - 1, :, place],
                    z_recv.at[j - 1, :, place],
                    mz_send.at[n - strips[0]],
                    mz_recv.at[n - strips[0]],
                    peers[j - 1],
                )

    def weights_here(p):
        for k in (2 * p, 2 * p + 1):
            local[1 + k].wait()
            swap[k].wait_recv()

    local[0].wait()
    tp[0, 0].wait_recv()
    weights_here(0)
    multiply_block(x, ny * (wide // TILE), wide // TILE)
    send_part(0, 0, x, at_128(ny * wide, wide))
    offer(3)
    arrive_across(0)
    tp[0, 1].wait_recv()
    multiply_block(nx, ny * (wide // TILE), wide // TILE)
    send_part(1, 0, nx, at_128(ny * wide, wide))
    weights_here(1)
    multiply(0, last // TILE, 2 * left // TILE)
    send_part(2, 0, ny, slice(last, units))
    weights_here(2)
    multiply(0, y * (wide // TILE), wide // TILE, keep_both=True)
    offer(1)
    sum_weights()
    activate(0)
    across(0)
    arrive(2)
    activate(1)
    across(1)
    activate(2)
    across(2)
    arrive_across(2)
    gate_and_up(2)
    send_rest(2)
    total_weights()
    hand_over(0)
    hand_over(1)
    hand_over(2)
    arrive(3)
    activate(5)
    across(5)
    arrive_across(3)
    gate_and_up(3)
    send_rest(3)
    arrive(1)
    activate(6)
    across(6)
    down_across()
    down_own()
    arrive_across(1)
    gate_and_up(1)
    activate(7)
    across(7)
    send_rest(1)
    activate(8)
    across(8)
    hand_over(5)
    hand_over(6)
    down_part(2)
    activate(3)
    across(3)
    checks(0)
    add_across(0)
    hand_over(7)
    hand_over(8)
    down_part(3)
    add_across(2)
    activate(4)
    across(4)
    checks(2)
    checks(3)
    add_across(3)
    hand_over(3)
    hand_over(4)
    down_part(1, column_terms=True)
    add_tokens(1)

    columns = jnp.sum(column_sums[...], axis=0, keepdims=True)
    for j in range(4):
        for b in range(2):
            for k in range(width // 128):
                small_send[j, b, k : k + 1, :] = columns[:, k * 128 : (k + 1) * 128]
    me = x * 4 + z
    small_recv[me] = small_send[0, x]
    small = [
        send(
            small_send.at[slot[0], slot[1]],
            small_recv.at[me],
            sm_send.at[k],
            sm_recv.at[k],
            peers[k],
        )
        for k, slot in enumerate(small_slots)
    ]
    add_across(1)
    for copy in small:
        copy.wait_recv()
    total = small_recv[0]
    for k in range(1, 8):
        total = total + small_recv[k]
    col_ref[...] = total[0:8] / math.sqrt(total_tokens)
    row_ref[...] = total[8:16] / math.sqrt(model_width)
    for j in range(1, 4):
        for n, _ in strips_of(j):
            mz[n].wait_recv()
    mixed_ref[...] = (
        own_sum[...]
        + z_recv[0].astype(jnp.float32)
        + z_recv[1].astype(jnp.float32)
        + z_recv[2].astype(jnp.float32)
    ).astype(jnp.bfloat16)
    for copy in sent:
        copy.wait_send()


def write_results(mixed_ref, col_ref, row_ref, mixed_out, col_out, row_out):
    mixed_out[...] = mixed_ref[...]
    for k in range(col_ref.shape[0]):
        col_out[pl.ds(k * 128, 128)] = col_ref[k]
    row_out[...] = row_ref[0, 0 : row_out.shape[0]]


def per_device_kernel(tokens, gate_up, down_weight):
    block, width = tokens.shape
    units = down_weight.shape[0]
    half = units // 2
    total_tokens = block * lax.axis_size(("dp", "col"))
    model_width = width * lax.axis_size("row")
    dma = pltpu.SemaphoreType.DMA
    bf16, f32 = jnp.bfloat16, jnp.float32
    sems = []
    for count in (6, 3, 4, 8, 9, 9, 9, 9, 12, 10, 3, 7):
        sems += [dma((count,)), dma((count,))]
    mixed, col, row = pl.pallas_call(
        functools.partial(kernel, total_tokens, model_width),
        out_shape=(
            jax.ShapeDtypeStruct((block, width), bf16),
            jax.ShapeDtypeStruct((8, 128), f32),
            jax.ShapeDtypeStruct((8, 128), f32),
        ),
        in_specs=[pl.BlockSpec(memory_space=pl.ANY)] * 3,
        out_specs=(pl.BlockSpec(memory_space=pltpu.VMEM),) * 3,
        scratch_shapes=[
            pltpu.VMEM((2, width, units), bf16),
            pltpu.VMEM((units, width), bf16),
            pltpu.VMEM((4, 2, 2, block, width), bf16),
            pltpu.VMEM((4, 2, block, units), f32),
            pltpu.VMEM((4, 2, block, units), bf16),
            pltpu.VMEM((4, 2, block, units), bf16),
            pltpu.VMEM((4, 2, 2, block, half), bf16),
            pltpu.VMEM((4, 2, block, width), f32),
            pltpu.VMEM((4, 2, block, width), bf16),
            pltpu.VMEM((4, block, width), bf16),
            pltpu.VMEM((3, block, width), bf16),
            pltpu.VMEM((3, block, width), bf16),
            pltpu.VMEM((block, width), f32),
            pltpu.VMEM((2, 16, half), f32),
            pltpu.VMEM((4, 16, 128), f32),
            pltpu.VMEM((2, 8, half), bf16),
            pltpu.VMEM((4, 2, 16, 128), f32),
            pltpu.VMEM((8, 16, 128), f32),
            pltpu.VMEM((2, 16, half), bf16),
            pltpu.VMEM((8, width), f32),
            dma((8,)),
        ]
        + sems,
        compiler_params=pltpu.CompilerParams(
            collective_id=0, has_side_effects=True, vmem_limit_bytes=56 * 2**20
        ),
        name="swiglu_grid",
    )(tokens, gate_up, down_weight)
    return pl.pallas_call(
        write_results,
        out_shape=(
            jax.ShapeDtypeStruct((block, width), bf16),
            jax.ShapeDtypeStruct((width,), f32),
            jax.ShapeDtypeStruct((block,), f32),
        ),
        name="write_results",
    )(mixed, col, row)


def fits_kernel(mesh):
    return dict(mesh.shape) == {"dp": 2, "row": 4, "col": 4}


def solution(mesh):
    body = per_device_kernel if fits_kernel(mesh) else per_device
    placed = (P(("dp", "col"), "row"), P(None, "row", ("dp", "col")), P(("dp", "col"), "row"))
    return jax.shard_map(
        body,
        mesh=mesh,
        in_specs=placed,
        out_specs=(P(("dp", "col"), "row"), P("row"), P(("dp", "col"))),
        check_vma=False,
    )
```
